512 devices in a mesh: pass: 64 (over y, z_lo, core), qry: 8 (over x, z_hi).
Axes of the slice: x: 4, y: 4, z: 16 (z_hi: 2, z_lo: 8; z = z_hi * 8 + z_lo), core: 2. Of those that a mesh axis runs over, the one named last changes fastest.
Arguments:
- queries: bfloat16 [1024, 768], P(('pass', 'qry')), may hold values from -6 to 6
- passages: bfloat16 [65536, 768], P(('pass', 'qry')), may hold values from -32 to 32
- teacher: bfloat16 [1024, 65536], P(('pass', 'qry')), may hold values from -16 to 320
Outputs:
- query_grad: float32 [1024, 768], P(('pass', 'qry'))
- passage_grad: float32 [65536, 768], P(('pass', 'qry'))
The draws below stay inside these ranges and needn't reach their ends.
All inputs are finite; a program needn't handle non-finite values.
Results may differ from the reference program's by a relative error of at most 0.0003.
Values may be sent and summed in bfloat16 or wider, within the bound.
No kernel may reach another device: no remote copies, remote signals or barrier semaphores. Data moves between devices by JAX's collectives and lax.ppermute only.
A program may use at most 64 MiB of HBM per device.

```python
import jax
import jax.numpy as jnp
from jax import lax

D = 768
NQ = 1024
NP = 65536


def base_queries(key):
    return jnp.clip(jax.random.normal(jax.random.fold_in(key, 11), (NQ, D), jnp.float32), -6.0, 6.0)


def draw_queries(key, part):
    key = jax.random.fold_in(key, 2)
    return base_queries(key).astype(jnp.bfloat16)


def draw_passages(key, part):
    key = jax.random.fold_in(key, 3)
    first_key = jax.random.fold_in(key, 0)
    pool = jnp.clip(jax.random.normal(first_key, (NP, D), jnp.float32), -6.0, 6.0)
    return pool.astype(jnp.bfloat16)


def draw_teacher(key, part):
    key = jax.random.fold_in(key, 5)
    first_key = jax.random.fold_in(key, 0)
    logits = jnp.clip(3.0 * jax.random.normal(first_key, (NQ, NP), jnp.float32), -15.0, 15.0)
    return logits.astype(jnp.bfloat16)


def setup_inputs(seed: int = 0) -> dict:
    seeds = jax.random.split(jax.random.key(seed), 4)
    return {
        "queries": draw_queries(jax.random.fold_in(seeds[3], 71), 0),
        "passages": draw_passages(jax.random.fold_in(seeds[3], 71), 0),
        "teacher": draw_teacher(jax.random.fold_in(seeds[3], 71), 0),
    }


logit_scale = 0.125


def row_softmax(values):
    top_value = jnp.max(values, axis=1, keepdims=True)
    lifted = jnp.exp(values - top_value)
    return lifted / jnp.sum(lifted, axis=1, keepdims=True)


def reference(queries, passages, teacher):
    block_rows = min(NQ, 64)
    pool_wide = passages.astype(jnp.float32)

    def advance(running, block_index):
        start = (block_index * block_rows).astype(jnp.int32)
        query_block = lax.dynamic_slice_in_dim(queries, start, block_rows, 0)
        teach_block = lax.dynamic_slice_in_dim(teacher, start, block_rows, 0).astype(jnp.float32)
        student = logit_scale * lax.dot_general(query_block, passages, (((1,), (1,)), ((), ())), preferred_element_type=jnp.float32)
        gap = logit_scale * (row_softmax(student) - row_softmax(teach_block))
        query_part = jnp.dot(gap, pool_wide, precision=lax.Precision.HIGHEST, preferred_element_type=jnp.float32)
        running = running + lax.dot_general(gap, query_block.astype(jnp.float32), (((0,), (0,)), ((), ())), precision=lax.Precision.HIGHEST, preferred_element_type=jnp.float32)
        return running, query_part

    passage_grad, query_parts = lax.scan(advance, jnp.zeros((NP, D), jnp.float32), jnp.arange(NQ // block_rows, dtype=jnp.int32))
    return query_parts.reshape(NQ, D), passage_grad
```

```python
import jax
import jax.numpy as jnp
from jax import lax
from jax.sharding import Mesh
from jax.sharding import PartitionSpec as P

logit_scale = 0.125
names = ("y", "zl", "core", "x", "zh")
sizes = (4, 8, 2, 4, 2)
z_axes = ("zh", "zl")
group_axes = ("core", "x")
lane = 128
f32 = jnp.float32
bf16 = jnp.bfloat16


def exchange(values, axes):
    return lax.all_to_all(values, axes, 0, 0, tiled=True)


def split_dot(weights, exact, dims):
    high = lax.reduce_precision(weights, 8, 7)
    low = weights - high
    return lax.dot_general(
        high.astype(bf16), exact, dims, preferred_element_type=f32
    ) + lax.dot_general(low.astype(bf16), exact, dims, preferred_element_type=f32)


def combine(top, total, axis):
    high = jnp.max(top, axis=axis, keepdims=True)
    weight = jnp.exp(top - high)
    return weight, jnp.squeeze(high, axis), jnp.sum(weight * total, axis=axis)


def per_device(queries, passages, teacher):
    own, dim = queries.shape
    pool = passages.shape[0]
    ny, nzl, nc, nx, nzh = (lax.axis_size(a) for a in names)
    nz, group = nzh * nzl, nc * nx
    fold = dim // lane

    tiles = teacher.reshape(own, ny, nzl, nc, nx, nzh, pool).transpose(5, 2, 1, 0, 3, 4, 6)
    tiles = tiles.reshape(nz, ny * own * group, pool)
    rows = jnp.broadcast_to(queries.reshape(1, own * fold, lane), (nz, own * fold, lane))
    got = exchange(jnp.concatenate([tiles, rows], axis=1), z_axes)
    cut = ny * own * group
    tiles = got[:, :cut].reshape(nz, ny, own * group, pool).transpose(1, 0, 2, 3)
    tiles = tiles.reshape(ny, nz * own * group, pool)
    rows = jnp.broadcast_to(got[:, cut:].reshape(1, nz * own * fold, lane), (ny, nz * own * fold, lane))
    got = exchange(jnp.concatenate([tiles, rows], axis=1), "y")
    cut = nz * own * group
    count = ny * nz * own
    logits = got[:, :cut].reshape(count, group * pool)
    block = got[:, cut:].reshape(count, dim)

    shared = lax.all_gather(passages, group_axes, axis=0, tiled=True)
    all_rows = lax.all_gather(block, group_axes, axis=0, tiled=True)
    own_logits = exchange(logits.reshape(count, group, pool).transpose(1, 0, 2), group_axes)
    own_logits = own_logits.reshape(group * count, pool)

    student = logit_scale * lax.dot_general(
        block, shared, (((1,), (1,)), ((), ())), preferred_element_type=f32
    )

    def local(values):
        top = jnp.max(values, axis=1, keepdims=True)
        lifted = jnp.exp(values - top)
        part = split_dot(lifted, shared, (((1,), (0,)), ((), ())))
        return part, top[:, 0], jnp.sum(lifted, axis=1)

    part_s, top_s, sum_s = local(student)
    part_t, top_t, sum_t = local(logits.astype(f32))
    parts = jnp.concatenate([part_s, part_t], axis=1)
    stats = jnp.stack([top_s, sum_s, top_t, sum_t])

    def reduce_over(parts, stats, axes, n, place):
        width = parts.shape[0] // n
        sent = jnp.concatenate(
            [
                parts.reshape(n, width * 2 * fold, lane),
                jnp.broadcast_to(stats.reshape(1, -1, lane), (n, stats.size // lane, lane)),
            ],
            axis=1,
        )
        got = exchange(sent, axes)
        parts = got[:, : width * 2 * fold].reshape(n, width, 2, dim)
        stats = got[:, width * 2 * fold :].reshape(n, 4, -1)
        weight_s, top_s, sum_s = combine(stats[:, 0], stats[:, 1], 0)
        weight_t, top_t, sum_t = combine(stats[:, 2], stats[:, 3], 0)
        weight_s = lax.dynamic_slice_in_dim(weight_s, place, width, 1)
        weight_t = lax.dynamic_slice_in_dim(weight_t, place, width, 1)
        part_s = jnp.sum(weight_s[:, :, None] * parts[:, :, 0], axis=0)
        part_t = jnp.sum(weight_t[:, :, None] * parts[:, :, 1], axis=0)
        return part_s, part_t, jnp.stack([top_s, sum_s, top_t, sum_t])

    y_at = lax.axis_index("y") * (nz * own)
    z_at = y_at + lax.axis_index(z_axes) * own
    part_s, part_t, stats = reduce_over(parts, stats, "y", ny, y_at)
    part_s, part_t, stats = reduce_over(
        jnp.concatenate([part_s, part_t], axis=1), stats, z_axes, nz, z_at
    )
    mine = lax.dynamic_slice_in_dim(stats, z_at, own, 1)
    query_grad = logit_scale * (part_s / mine[1][:, None] - part_t / mine[3][:, None])

    every = exchange(jnp.broadcast_to(stats[None], (group,) + stats.shape), group_axes)
    every = every.transpose(1, 0, 2).reshape(4, group * count)
    scores = logit_scale * lax.dot_general(
        passages, all_rows, (((1,), (1,)), ((), ())), preferred_element_type=f32
    )
    grad = logit_scale * (
        jnp.exp(scores - every[0]) / every[1]
        - jnp.exp(own_logits.T.astype(f32) - every[2]) / every[3]
    )
    passage_grad = split_dot(grad, all_rows, (((1,), (0,)), ((), ())))
    return query_grad, passage_grad


def solution(mesh):
    shape = sizes if mesh.devices.size == 512 else (2,) * 5
    fine = Mesh(mesh.devices.reshape(shape), names)
    placed = P(names, None)
    return jax.shard_map(
        per_device,
        mesh=fine,
        in_specs=(placed, placed, placed),
        out_specs=(placed, placed),
        check_vma=False,
    )
```

```python
import jax
import jax.numpy as jnp
from jax import lax
from jax.sharding import Mesh
from jax.sharding import PartitionSpec as P

logit_scale = 0.125
names = ("y", "zl", "core", "x", "zh")
sizes = (4, 8, 2, 4, 2)
z_axes = ("zh", "zl")
group_axes = ("core", "x")
lane = 128
f32 = jnp.float32
bf16 = jnp.bfloat16


def exchange(values, axes):
    return lax.all_to_all(values, axes, 0, 0, tiled=True)


def split_dot(weights, exact, dims):
    high = lax.reduce_precision(weights, 8, 7)
    low = weights - high
    return lax.dot_general(
        high.astype(bf16), exact, dims, preferred_element_type=f32
    ) + lax.dot_general(low.astype(bf16), exact, dims, preferred_element_type=f32)


def combine(top, total, axis):
    high = jnp.max(top, axis=axis, keepdims=True)
    weight = jnp.exp(top - high)
    return weight, jnp.squeeze(high, axis), jnp.sum(weight * total, axis=axis)


def per_device(queries, passages, teacher):
    own, dim = queries.shape
    pool = passages.shape[0]
    ny, nzl, nc, nx, nzh = (lax.axis_size(a) for a in names)
    nz, group = nzh * nzl, nc * nx
    fold = dim // lane

    shared = exchange(jnp.broadcast_to(passages[None], (group, pool, dim)), group_axes)
    shared = shared.reshape(group * pool, dim)

    tiles = teacher.reshape(own, ny, nzl, nc, nx, nzh, pool).transpose(5, 2, 1, 0, 3, 4, 6)
    tiles = tiles.reshape(nz, ny * own * group, pool)
    rows = jnp.broadcast_to(queries.reshape(1, own * fold, lane), (nz, own * fold, lane))
    got = exchange(jnp.concatenate([tiles, rows], axis=1), z_axes)
    cut = ny * own * group
    tiles = got[:, :cut].reshape(nz, ny, own * group, pool).transpose(1, 0, 2, 3)
    tiles = tiles.reshape(ny, nz * own * group, pool)
    rows = jnp.broadcast_to(got[:, cut:].reshape(1, nz * own * fold, lane), (ny, nz * own * fold, lane))
    got = exchange(jnp.concatenate([tiles, rows], axis=1), "y")
    cut = nz * own * group
    count = ny * nz * own
    logits = got[:, :cut].reshape(count, group * pool)
    block = got[:, cut:].reshape(count, dim)

    rows = jnp.broadcast_to(block[None], (group, count, dim))
    tiles = logits.reshape(count, group, pool).transpose(1, 0, 2)
    every_row = exchange(jnp.concatenate([rows, tiles], axis=2), group_axes)
    every_row = every_row.reshape(group * count, dim + pool)
    all_rows, own_logits = every_row[:, :dim], every_row[:, dim:]

    student = logit_scale * lax.dot_general(
        block, shared, (((1,), (1,)), ((), ())), preferred_element_type=f32
    )

    def local(values):
        top = jnp.max(values, axis=1, keepdims=True)
        lifted = jnp.exp(values - top)
        part = split_dot(lifted, shared, (((1,), (0,)), ((), ())))
        return part, top[:, 0], jnp.sum(lifted, axis=1)

    part_s, top_s, sum_s = local(student)
    part_t, top_t, sum_t = local(logits.astype(f32))
    parts = jnp.concatenate([part_s, part_t], axis=1)
    stats = jnp.stack([top_s, sum_s, top_t, sum_t])

    def reduce_over(parts, stats, axes, n, place):
        width = parts.shape[0] // n
        extra = -(-stats.size // width)
        extra += -extra % lane
        spread = jnp.pad(stats.reshape(-1, extra), ((0, width - stats.size // extra), (0, 0)))
        sent = jnp.concatenate([parts.reshape(n, width, 2 * dim), jnp.broadcast_to(spread, (n, width, extra))], axis=2)
        got = exchange(sent, axes)
        parts = got[:, :, : 2 * dim]
        stats = got[:, : stats.size // extra, 2 * dim :].reshape(n, 4, -1)
        weight_s, top_s, sum_s = combine(stats[:, 0], stats[:, 1], 0)
        weight_t, top_t, sum_t = combine(stats[:, 2], stats[:, 3], 0)
        weight_s = lax.dynamic_slice_in_dim(weight_s, place, width, 1)
        weight_t = lax.dynamic_slice_in_dim(weight_t, place, width, 1)
        part_s = jnp.sum(weight_s[:, :, None] * parts[:, :, :dim], axis=0)
        part_t = jnp.sum(weight_t[:, :, None] * parts[:, :, dim:], axis=0)
        return part_s, part_t, jnp.stack([top_s, sum_s, top_t, sum_t])

    y_at = lax.axis_index("y") * (nz * own)
    z_at = y_at + lax.axis_index(z_axes) * own
    part_s, part_t, stats = reduce_over(parts, stats, "y", ny, y_at)
    part_s, part_t, stats = reduce_over(
        jnp.concatenate([part_s, part_t], axis=1), stats, z_axes, nz, z_at
    )
    mine = lax.dynamic_slice_in_dim(stats, z_at, own, 1)
    query_grad = logit_scale * (part_s / mine[1][:, None] - part_t / mine[3][:, None])

    scores = logit_scale * lax.dot_general(
        passages, all_rows, (((1,), (1,)), ((), ())), preferred_element_type=f32
    )
    stats, scores = lax.optimization_barrier((stats, scores))
    every = exchange(jnp.broadcast_to(stats[None], (group,) + stats.shape), group_axes)
    every = every.transpose(1, 0, 2).reshape(4, group * count)
    grad = logit_scale * (
        jnp.exp(scores - every[0]) / every[1]
        - jnp.exp(own_logits.T.astype(f32) - every[2]) / every[3]
    )
    passage_grad = split_dot(grad, all_rows, (((1,), (0,)), ((), ())))
    return query_grad, passage_grad


def solution(mesh):
    shape = sizes if mesh.devices.size == 512 else (2,) * 5
    fine = Mesh(mesh.devices.reshape(shape), names)
    placed = P(names, None)
    return jax.shard_map(
        per_device,
        mesh=fine,
        in_specs=(placed, placed, placed),
        out_specs=(placed, placed),
        check_vma=False,
    )
```

```python
import jax
import jax.numpy as jnp
from jax import lax
from jax.sharding import Mesh
from jax.sharding import PartitionSpec as P

logit_scale = 0.125
names = ("y", "zl", "core", "x", "zh")
sizes = (4, 8, 2, 4, 2)
z_axes = ("zh", "zl")
group_axes = ("core", "x")
lane = 128
f32 = jnp.float32
bf16 = jnp.bfloat16


def exchange(values, axes):
    return lax.all_to_all(values, axes, 0, 0, tiled=True)


def from_next(values, axis, step):
    n = lax.axis_size(axis)
    return lax.ppermute(values, axis, [(i, (i - step) % n) for i in range(n)])


def rolled(values, axis, dim):
    twice = jnp.concatenate([values, values], axis=dim)
    return lax.dynamic_slice_in_dim(twice, lax.axis_index(axis), lax.axis_size(axis), dim)


def split_dot(weights, exact, dims):
    high = lax.reduce_precision(weights, 8, 7)
    low = weights - high
    return lax.dot_general(
        high.astype(bf16), exact, dims, preferred_element_type=f32
    ) + lax.dot_general(low.astype(bf16), exact, dims, preferred_element_type=f32)


def combine(top, total, axis):
    high = jnp.max(top, axis=axis, keepdims=True)
    weight = jnp.exp(top - high)
    return weight, jnp.squeeze(high, axis), jnp.sum(weight * total, axis=axis)


def per_device(queries, passages, teacher):
    own, dim = queries.shape
    pool = passages.shape[0]
    ny, nzl, nc, nx, nzh = (lax.axis_size(a) for a in names)
    nz, group = nzh * nzl, nc * nx
    fold = dim // lane

    near = [from_next(passages, "x", k) for k in range(1, nx)]

    tiles = teacher.reshape(own, ny, nzl, nc, nx, nzh, pool)
    tiles = rolled(rolled(tiles, "x", 4), "core", 3).transpose(5, 2, 1, 0, 3, 4, 6)
    tiles = tiles.reshape(nz, ny * own * group, pool)
    rows = jnp.broadcast_to(queries.reshape(1, own * fold, lane), (nz, own * fold, lane))
    got = exchange(jnp.concatenate([tiles, rows], axis=1), z_axes)
    got, *near = lax.optimization_barrier((got, *near))
    near = jnp.stack([passages, *near])
    far = from_next(near, "core", 1)
    cut = ny * own * group
    tiles = got[:, :cut].reshape(nz, ny, own * group, pool).transpose(1, 0, 2, 3)
    tiles = tiles.reshape(ny, nz * own * group, pool)
    rows = jnp.broadcast_to(got[:, cut:].reshape(1, nz * own * fold, lane), (ny, nz * own * fold, lane))
    got = exchange(jnp.concatenate([tiles, rows], axis=1), "y")
    cut = nz * own * group
    count = ny * nz * own
    logits = got[:, :cut].reshape(count, group * pool)
    block = got[:, cut:].reshape(count, dim)
    shared = jnp.concatenate([near, far]).reshape(group * pool, dim)

    def columns(c, k):
        return logits[:, (c * nx + k) * pool :][:, :pool]

    rows = [
        jnp.concatenate([block, columns(0, -k % nx), columns(1, -k % nx)], axis=1) for k in range(nx)
    ]
    rows = [rows[0]] + [from_next(rows[k], "x", k) for k in range(1, nx)]

    student = logit_scale * lax.dot_general(
        block, shared, (((1,), (1,)), ((), ())), preferred_element_type=f32
    )

    def local(values):
        top = jnp.max(values, axis=1, keepdims=True)
        lifted = jnp.exp(values - top)
        part = split_dot(lifted, shared, (((1,), (0,)), ((), ())))
        return part, top[:, 0], jnp.sum(lifted, axis=1)

    part_s, top_s, sum_s = local(student)
    part_t, top_t, sum_t = local(logits.astype(f32))
    parts = jnp.concatenate([part_s, part_t], axis=1)
    stats = jnp.stack([top_s, sum_s, top_t, sum_t])

    def reduce_over(parts, stats, axes, n, place):
        width = parts.shape[0] // n
        extra = -(-stats.size // width)
        extra += -extra % lane
        spread = jnp.pad(stats.reshape(-1, extra), ((0, width - stats.size // extra), (0, 0)))
        sent = jnp.concatenate([parts.reshape(n, width, 2 * dim), jnp.broadcast_to(spread, (n, width, extra))], axis=2)
        got = exchange(sent, axes)
        parts = got[:, :, : 2 * dim]
        stats = got[:, : stats.size // extra, 2 * dim :].reshape(n, 4, -1)
        weight_s, top_s, sum_s = combine(stats[:, 0], stats[:, 1], 0)
        weight_t, top_t, sum_t = combine(stats[:, 2], stats[:, 3], 0)
        weight_s = lax.dynamic_slice_in_dim(weight_s, place, width, 1)
        weight_t = lax.dynamic_slice_in_dim(weight_t, place, width, 1)
        part_s = jnp.sum(weight_s[:, :, None] * parts[:, :, :dim], axis=0)
        part_t = jnp.sum(weight_t[:, :, None] * parts[:, :, dim:], axis=0)
        return part_s, part_t, jnp.stack([top_s, sum_s, top_t, sum_t])

    y_at = lax.axis_index("y") * (nz * own)
    z_at = y_at + lax.axis_index(z_axes) * own
    part_s, part_t, stats = reduce_over(parts, stats, "y", ny, y_at)
    part_s, part_t, stats, *rows = lax.optimization_barrier((part_s, part_t, stats, *rows))
    kept = jnp.stack([r[:, : dim + pool] for r in rows])
    sent = jnp.stack([jnp.concatenate([r[:, :dim], r[:, dim + pool :]], axis=1) for r in rows])
    every_row = jnp.concatenate([kept, from_next(sent, "core", 1)]).reshape(group * count, dim + pool)
    all_rows, own_logits = every_row[:, :dim], every_row[:, dim:]
    part_s, part_t, stats = reduce_over(
        jnp.concatenate([part_s, part_t], axis=1), stats, z_axes, nz, z_at
    )
    mine = lax.dynamic_slice_in_dim(stats, z_at, own, 1)
    query_grad = logit_scale * (part_s / mine[1][:, None] - part_t / mine[3][:, None])

    def lifted(values):
        top = jnp.max(values, axis=0)
        return jnp.exp(values - top), top

    scores, high_s = lifted(
        logit_scale
        * lax.dot_general(passages, all_rows, (((1,), (1,)), ((), ())), preferred_element_type=f32)
    )
    wanted, high_t = lifted(own_logits.T.astype(f32))
    stats, scores, wanted, high_s, high_t = lax.optimization_barrier(
        (stats, scores, wanted, high_s, high_t)
    )
    every = exchange(jnp.broadcast_to(stats[None], (group,) + stats.shape), group_axes)
    every = rolled(rolled(every.reshape(nc, nx, 4, count), "x", 1), "core", 0)
    every = every.transpose(2, 0, 1, 3).reshape(4, group * count)
    grad = (logit_scale * jnp.exp(high_s - every[0]) / every[1]) * scores - (
        logit_scale * jnp.exp(high_t - every[2]) / every[3]
    ) * wanted
    passage_grad = split_dot(grad, all_rows, (((1,), (0,)), ((), ())))
    return query_grad, passage_grad


def solution(mesh):
    shape = sizes if mesh.devices.size == 512 else (2,) * 5
    fine = Mesh(mesh.devices.reshape(shape), names)
    placed = P(names, None)
    return jax.shard_map(
        per_device,
        mesh=fine,
        in_specs=(placed, placed, placed),
        out_specs=(placed, placed),
        check_vma=False,
    )
```

```python
import jax
import jax.numpy as jnp
from jax import lax
from jax.sharding import Mesh
from jax.sharding import PartitionSpec as P

logit_scale = 0.125
names = ("y", "zl", "core", "x", "zh")
sizes = (4, 8, 2, 4, 2)
z_axes = ("zh", "zl")
group_axes = ("core", "x")
lane = 128
f32 = jnp.float32
bf16 = jnp.bfloat16


def exchange(values, axes):
    return lax.all_to_all(values, axes, 0, 0, tiled=True)


def from_next(values, axis, step):
    n = lax.axis_size(axis)
    return lax.ppermute(values, axis, [(i, (i - step) % n) for i in range(n)])


def rolled(values, axis, dim):
    twice = jnp.concatenate([values, values], axis=dim)
    return lax.dynamic_slice_in_dim(twice, lax.axis_index(axis), lax.axis_size(axis), dim)


def split_dot(weights, exact, dims):
    high = lax.reduce_precision(weights, 8, 7)
    low = weights - high
    return lax.dot_general(
        high.astype(bf16), exact, dims, preferred_element_type=f32
    ) + lax.dot_general(low.astype(bf16), exact, dims, preferred_element_type=f32)


def combine(top, total, axis):
    high = jnp.max(top, axis=axis, keepdims=True)
    weight = jnp.exp(top - high)
    return weight, jnp.squeeze(high, axis), jnp.sum(weight * total, axis=axis)


def per_device(queries, passages, teacher):
    own, dim = queries.shape
    pool = passages.shape[0]
    ny, nzl, nc, nx, nzh = (lax.axis_size(a) for a in names)
    nz, group = nzh * nzl, nc * nx
    fold = dim // lane

    near = [from_next(passages, "x", k) for k in range(1, nx)]

    tiles = teacher.reshape(own, ny, nzl, nc, nx, nzh, pool)
    tiles = rolled(rolled(tiles, "x", 4), "core", 3).transpose(5, 2, 1, 0, 3, 4, 6)
    tiles = tiles.reshape(nz, ny * own * group, pool)
    rows = jnp.broadcast_to(queries.reshape(1, own * fold, lane), (nz, own * fold, lane))
    got = exchange(jnp.concatenate([tiles, rows], axis=1), z_axes)
    got, *near = lax.optimization_barrier((got, *near))
    near = jnp.stack([passages, *near])
    far = from_next(near, "core", 1)
    cut = ny * own * group
    tiles = got[:, :cut].reshape(nz, ny, own * group, pool).transpose(1, 0, 2, 3)
    tiles = tiles.reshape(ny, nz * own * group, pool)
    rows = jnp.broadcast_to(got[:, cut:].reshape(1, nz * own * fold, lane), (ny, nz * own * fold, lane))
    got = exchange(jnp.concatenate([tiles, rows], axis=1), "y")
    cut = nz * own * group
    count = ny * nz * own
    logits = got[:, :cut].reshape(count, group * pool)
    block = got[:, cut:].reshape(count, dim)
    shared = jnp.concatenate([near, far]).reshape(group * pool, dim)

    def columns(c, k):
        return logits[:, (c * nx + k) * pool :][:, :pool]

    rows = [
        jnp.concatenate([block, columns(0, -k % nx), columns(1, -k % nx)], axis=1) for k in range(nx)
    ]
    rows = [rows[0]] + [from_next(rows[k], "x", k) for k in range(1, nx)]

    student = logit_scale * lax.dot_general(
        block, shared, (((1,), (1,)), ((), ())), preferred_element_type=f32
    )

    def local(values):
        top = jnp.max(values, axis=1, keepdims=True)
        lifted = jnp.exp(values - top)
        part = split_dot(lifted, shared, (((1,), (0,)), ((), ())))
        return part, top[:, 0], jnp.sum(lifted, axis=1)

    part_s, top_s, sum_s = local(student)
    part_t, top_t, sum_t = local(logits.astype(f32))
    parts = jnp.concatenate([part_s, part_t], axis=1)
    stats = jnp.stack([top_s, sum_s, top_t, sum_t])

    def pack(parts, stats, n):
        width = parts.shape[0] // n
        extra = -(-stats.size // width)
        extra += -extra % lane
        spread = jnp.pad(stats.reshape(-1, extra), ((0, width - stats.size // extra), (0, 0)))
        spread = jnp.broadcast_to(spread, (n, width, extra))
        return jnp.concatenate([parts.reshape(n, width, 2 * dim), spread], axis=2)

    def unpack(got, place):
        n, width, full = got.shape
        extra = full - 2 * dim
        stats = got[:, : 4 * count // extra, 2 * dim :].reshape(n, 4, count)
        weight_s, top_s, sum_s = combine(stats[:, 0], stats[:, 1], 0)
        weight_t, top_t, sum_t = combine(stats[:, 2], stats[:, 3], 0)
        weight_s = lax.dynamic_slice_in_dim(weight_s, place, width, 1)
        weight_t = lax.dynamic_slice_in_dim(weight_t, place, width, 1)
        part_s = jnp.sum(weight_s[:, :, None] * got[:, :, :dim], axis=0)
        part_t = jnp.sum(weight_t[:, :, None] * got[:, :, dim : 2 * dim], axis=0)
        return part_s, part_t, jnp.stack([top_s, sum_s, top_t, sum_t])

    y_at = lax.axis_index("y") * (nz * own)
    z_at = y_at + lax.axis_index(z_axes) * own
    part_s, part_t, stats = unpack(exchange(pack(parts, stats, ny), "y"), y_at)
    sent = pack(jnp.concatenate([part_s, part_t], axis=1), stats, nz)
    got = exchange(sent, z_axes)
    *rows, _ = lax.optimization_barrier((*rows, sent))
    kept = jnp.stack([r[:, : dim + pool] for r in rows])
    away = jnp.stack([jnp.concatenate([r[:, :dim], r[:, dim + pool :]], axis=1) for r in rows])
    every_row = jnp.concatenate([kept, from_next(away, "core", 1)]).reshape(group * count, dim + pool)
    all_rows, own_logits = every_row[:, :dim], every_row[:, dim:]
    part_s, part_t, stats = unpack(got, z_at)
    mine = lax.dynamic_slice_in_dim(stats, z_at, own, 1)
    query_grad = logit_scale * (part_s / mine[1][:, None] - part_t / mine[3][:, None])

    def lifted(values):
        top = jnp.max(values, axis=0)
        return jnp.exp(values - top), top

    scores, high_s = lifted(
        logit_scale
        * lax.dot_general(passages, all_rows, (((1,), (1,)), ((), ())), preferred_element_type=f32)
    )
    wanted, high_t = lifted(own_logits.T.astype(f32))
    stats, scores, wanted, high_s, high_t = lax.optimization_barrier(
        (stats, scores, wanted, high_s, high_t)
    )
    every = exchange(jnp.broadcast_to(stats[None], (group,) + stats.shape), group_axes)
    every = rolled(rolled(every.reshape(nc, nx, 4, count), "x", 1), "core", 0)
    every = every.transpose(2, 0, 1, 3).reshape(4, group * count)
    grad = (logit_scale * jnp.exp(high_s - every[0]) / every[1]) * scores - (
        logit_scale * jnp.exp(high_t - every[2]) / every[3]
    ) * wanted
    passage_grad = split_dot(grad, all_rows, (((1,), (0,)), ((), ())))
    return query_grad, passage_grad


def solution(mesh):
    shape = sizes if mesh.devices.size == 512 else (2,) * 5
    fine = Mesh(mesh.devices.reshape(shape), names)
    placed = P(names, None)
    return jax.shard_map(
        per_device,
        mesh=fine,
        in_specs=(placed, placed, placed),
        out_specs=(placed, placed),
        check_vma=False,
    )
```

```python
import functools

import jax
import jax.numpy as jnp
from jax import lax
from jax.experimental import pallas as pl
from jax.experimental.pallas import tpu as pltpu
from jax.sharding import Mesh
from jax.sharding import PartitionSpec as P

logit_scale = 0.125
names = ("y", "zl", "core", "x", "zh")
sizes = (4, 8, 2, 4, 2)
z_axes = ("zh", "zl")
group_axes = ("core", "x")
lane = 128
f32 = jnp.float32
bf16 = jnp.bfloat16


def exchange(values, axes):
    return lax.all_to_all(values, axes, 0, 0, tiled=True)


def from_next(values, axis, step):
    n = lax.axis_size(axis)
    return lax.ppermute(values, axis, [(i, (i - step) % n) for i in range(n)])


def rolled(values, axis, dim):
    twice = jnp.concatenate([values, values], axis=dim)
    return lax.dynamic_slice_in_dim(twice, lax.axis_index(axis), lax.axis_size(axis), dim)


def split_dot(weights, exact, dims):
    high = lax.reduce_precision(weights, 8, 7)
    low = weights - high
    return lax.dot_general(
        high.astype(bf16), exact, dims, preferred_element_type=f32
    ) + lax.dot_general(low.astype(bf16), exact, dims, preferred_element_type=f32)


def combine(top, total, axis):
    high = jnp.max(top, axis=axis, keepdims=True)
    weight = jnp.exp(top - high)
    return weight, jnp.squeeze(high, axis), jnp.sum(weight * total, axis=axis)


def bf16_parts(values):
    high = values.astype(bf16)
    return high, (values - high.astype(f32)).astype(bf16)


def along_lanes(column):
    n = column.shape[0]
    at_row = lax.broadcasted_iota(jnp.int32, (n, n), 0)
    at_lane = lax.broadcasted_iota(jnp.int32, (n, n), 1)
    return jnp.sum(jnp.where(at_row == at_lane, column, 0.0), axis=0, keepdims=True)


def parts_kernel(nc, nx, place, got, near, far, sent, block, logits, wide, columns):
    ny, width, out = sent.shape
    count, dim = block.shape
    pool = logits.shape[2]
    group, fold = nc * nx, dim // lane
    cut = width * group
    for y in range(ny):
        wide[y * cut : (y + 1) * cut] = got[y, :cut].astype(f32)
    for i in range(group):
        columns[i] = wide[pl.ds(i, count, stride=group), :]
    for i in range(group):
        c, k = divmod(i, nx)
        logits[i] = columns[(place[0] + c) % nc * nx + (place[1] + k) % nx].astype(bf16)
    cut_rows = width * fold
    for y in range(ny):
        wide[y * cut_rows : (y + 1) * cut_rows] = got[y, cut:].astype(f32)
    for i in range(fold):
        block[:, i * lane : (i + 1) * lane] = wide[pl.ds(i, count, stride=fold), :].astype(bf16)

    rows = block[...]
    shared = near[...], far[...]
    student = [
        logit_scale * lax.dot_general(rows, p, (((1,), (1,)), ((), ())), preferred_element_type=f32)
        for p in shared
    ]
    taught = [
        jnp.concatenate([logits[c * nx + k].astype(f32) for k in range(nx)], axis=1) for c in range(nc)
    ]
    stats = []
    for at, values in enumerate((student, taught)):
        top = functools.reduce(jnp.maximum, [jnp.max(v, axis=1, keepdims=True) for v in values])
        total = jnp.zeros_like(top)
        part = jnp.zeros((count, dim), f32)
        for v, p in zip(values, shared):
            lifted = jnp.exp(v - top)
            total += jnp.sum(lifted, axis=1, keepdims=True)
            for piece in bf16_parts(lifted):
                part += jnp.dot(piece, p, preferred_element_type=f32)
        for y in range(ny):
            sent[y, :, at * dim : (at + 1) * dim] = part[y * width : (y + 1) * width]
        stats += [along_lanes(top), along_lanes(total)]
    spread = jnp.concatenate(stats + [jnp.zeros((width - 4, count), f32)], axis=0)
    for y in range(ny):
        sent[y, :, 2 * dim :] = spread


def local_parts(got, near, far, sizes):
    ny, width, nc, nx, pool, dim = sizes
    count, group = ny * width, nc * nx
    place = jnp.stack([lax.axis_index("core"), lax.axis_index("x")]).astype(jnp.int32)
    vmem = pl.BlockSpec(memory_space=pltpu.VMEM)
    return pl.pallas_call(
        functools.partial(parts_kernel, nc, nx),
        out_shape=(
            jax.ShapeDtypeStruct((ny, width, 2 * dim + count), f32),
            jax.ShapeDtypeStruct((count, dim), bf16),
            jax.ShapeDtypeStruct((group, count, pool), bf16),
        ),
        in_specs=[pl.BlockSpec(memory_space=pltpu.SMEM), vmem, vmem, vmem],
        out_specs=(vmem, vmem, vmem),
        scratch_shapes=[
            pltpu.VMEM((count * max(group, dim // lane), lane), f32),
            pltpu.VMEM((group, count, pool), f32),
        ],
        compiler_params=pltpu.CompilerParams(vmem_limit_bytes=24 * 2**20),
        cost_estimate=pl.CostEstimate(
            flops=10 * count * group * pool * dim,
            bytes_accessed=4 * 2**20,
            transcendentals=2 * count * group * pool,
        ),
    )(place, got, near.reshape(nx * pool, dim), far.reshape(nx * pool, dim))


def per_device(queries, passages, teacher):
    own, dim = queries.shape
    pool = passages.shape[0]
    ny, nzl, nc, nx, nzh = (lax.axis_size(a) for a in names)
    nz, group = nzh * nzl, nc * nx
    fold = dim // lane

    near = [from_next(passages, "x", k) for k in range(1, nx)]

    tiles = teacher.reshape(own, ny, nzl, nc, nx, nzh, pool)
    tiles = tiles.transpose(5, 2, 1, 0, 3, 4, 6)
    tiles = tiles.reshape(nz, ny * own * group, pool)
    rows = jnp.broadcast_to(queries.reshape(1, own * fold, lane), (nz, own * fold, lane))
    got = exchange(jnp.concatenate([tiles, rows], axis=1), z_axes)
    got, *near = lax.optimization_barrier((got, *near))
    cut = ny * own * group
    tiles = got[:, :cut].reshape(nz, ny, own * group, pool).transpose(1, 0, 2, 3)
    tiles = tiles.reshape(ny, nz * own * group, pool)
    rows = jnp.broadcast_to(got[:, cut:].reshape(1, nz * own * fold, lane), (ny, nz * own * fold, lane))
    sent = jnp.concatenate([tiles, rows], axis=1)
    got = exchange(sent, "y")
    *near, _ = lax.optimization_barrier((*near, sent))
    near = jnp.stack([passages, *near])
    far = from_next(near, "core", 1)
    count = ny * nz * own
    sent, block, logits = local_parts(got, near, far, (ny, nz * own, nc, nx, pool, dim))

    rows = [
        jnp.concatenate([block] + [logits[c * nx + -k % nx] for c in range(nc)], axis=1)
        for k in range(nx)
    ]
    rows = [rows[0]] + [from_next(rows[k], "x", k) for k in range(1, nx)]

    def pack(parts, stats, n):
        width = parts.shape[0] // n
        extra = -(-stats.size // width)
        extra += -extra % lane
        spread = jnp.pad(stats.reshape(-1, extra), ((0, width - stats.size // extra), (0, 0)))
        spread = jnp.broadcast_to(spread, (n, width, extra))
        return jnp.concatenate([parts.reshape(n, width, 2 * dim), spread], axis=2)

    def unpack(got, place):
        n, width, full = got.shape
        extra = full - 2 * dim
        stats = got[:, : 4 * count // extra, 2 * dim :].reshape(n, 4, count)
        weight_s, top_s, sum_s = combine(stats[:, 0], stats[:, 1], 0)
        weight_t, top_t, sum_t = combine(stats[:, 2], stats[:, 3], 0)
        weight_s = lax.dynamic_slice_in_dim(weight_s, place, width, 1)
        weight_t = lax.dynamic_slice_in_dim(weight_t, place, width, 1)
        part_s = jnp.sum(weight_s[:, :, None] * got[:, :, :dim], axis=0)
        part_t = jnp.sum(weight_t[:, :, None] * got[:, :, dim : 2 * dim], axis=0)
        return part_s, part_t, jnp.stack([top_s, sum_s, top_t, sum_t])

    y_at = lax.axis_index("y") * (nz * own)
    z_at = y_at + lax.axis_index(z_axes) * own
    part_s, part_t, stats = unpack(exchange(sent, "y"), y_at)
    sent = pack(jnp.concatenate([part_s, part_t], axis=1), stats, nz)
    got = exchange(sent, z_axes)
    *rows, _ = lax.optimization_barrier((*rows, sent))
    kept = jnp.stack([r[:, : dim + pool] for r in rows])
    away = jnp.stack([jnp.concatenate([r[:, :dim], r[:, dim + pool :]], axis=1) for r in rows])
    every_row = jnp.concatenate([kept, from_next(away, "core", 1)]).reshape(group * count, dim + pool)
    all_rows, own_logits = every_row[:, :dim], every_row[:, dim:]

    def lifted(values):
        top = jnp.max(values, axis=0)
        return jnp.exp(values - top), top

    scores, high_s = lifted(
        logit_scale
        * lax.dot_general(passages, all_rows, (((1,), (1,)), ((), ())), preferred_element_type=f32)
    )
    wanted, high_t = lifted(own_logits.T.astype(f32))
    got, scores, wanted, high_s, high_t = lax.optimization_barrier(
        (got, scores, wanted, high_s, high_t)
    )
    part_s, part_t, stats = unpack(got, z_at)
    mine = lax.dynamic_slice_in_dim(stats, z_at, own, 1)
    query_grad = logit_scale * (part_s / mine[1][:, None] - part_t / mine[3][:, None])

    every = exchange(jnp.broadcast_to(stats[None], (group,) + stats.shape), group_axes)
    every = rolled(rolled(every.reshape(nc, nx, 4, count), "x", 1), "core", 0)
    every = every.transpose(2, 0, 1, 3).reshape(4, group * count)
    grad = (logit_scale * jnp.exp(high_s - every[0]) / every[1]) * scores - (
        logit_scale * jnp.exp(high_t - every[2]) / every[3]
    ) * wanted
    passage_grad = split_dot(grad, all_rows, (((1,), (0,)), ((), ())))
    return query_grad, passage_grad


def solution(mesh):
    shape = sizes if mesh.devices.size == 512 else (2,) * 5
    fine = Mesh(mesh.devices.reshape(shape), names)
    placed = P(names, None)
    return jax.shard_map(
        per_device,
        mesh=fine,
        in_specs=(placed, placed, placed),
        out_specs=(placed, placed),
        check_vma=False,
    )
```

```python
import functools

import jax
import jax.numpy as jnp
from jax import lax
from jax.experimental import pallas as pl
from jax.experimental.pallas import tpu as pltpu
from jax.sharding import Mesh
from jax.sharding import PartitionSpec as P

logit_scale = 0.125
names = ("y", "zl", "core", "x", "zh")
sizes = (4, 8, 2, 4, 2)
z_axes = ("zh", "zl")
group_axes = ("core", "x")
lane = 128
f32 = jnp.float32
bf16 = jnp.bfloat16


def exchange(values, axes):
    return lax.all_to_all(values, axes, 0, 0, tiled=True)


def from_next(values, axis, step):
    n = lax.axis_size(axis)
    return lax.ppermute(values, axis, [(i, (i - step) % n) for i in range(n)])


def rolled(values, axis, dim):
    twice = jnp.concatenate([values, values], axis=dim)
    return lax.dynamic_slice_in_dim(twice, lax.axis_index(axis), lax.axis_size(axis), dim)


def split_dot(weights, exact, dims):
    high = lax.reduce_precision(weights, 8, 7)
    low = weights - high
    return lax.dot_general(
        high.astype(bf16), exact, dims, preferred_element_type=f32
    ) + lax.dot_general(low.astype(bf16), exact, dims, preferred_element_type=f32)


def combine(top, total, axis):
    high = jnp.max(top, axis=axis, keepdims=True)
    weight = jnp.exp(top - high)
    return weight, jnp.squeeze(high, axis), jnp.sum(weight * total, axis=axis)


def bf16_parts(values):
    high = values.astype(bf16)
    return high, (values - high.astype(f32)).astype(bf16)


def along_lanes(column):
    n = column.shape[0]
    at_row = lax.broadcasted_iota(jnp.int32, (n, n), 0)
    at_lane = lax.broadcasted_iota(jnp.int32, (n, n), 1)
    return jnp.sum(jnp.where(at_row == at_lane, column, 0.0), axis=0, keepdims=True)


def layout_kernel(nc, nx, place, got, block, high, low, stats, *rest):
    *rows, wide, columns = rest
    ny = got.shape[0]
    count, dim = block.shape
    group, fold = nc * nx, dim // lane
    width = count // ny
    cut = width * group
    cut_rows = width * fold
    for y in range(ny):
        wide[y * cut_rows : (y + 1) * cut_rows] = got[y, cut:].astype(f32)
    for i in range(fold):
        block[:, i * lane : (i + 1) * lane] = wide[pl.ds(i, count, stride=fold), :].astype(bf16)
    for y in range(ny):
        wide[y * cut : (y + 1) * cut] = got[y, :cut].astype(f32)
    for i in range(group):
        columns[i] = wide[pl.ds(i, count, stride=group), :]
    taught = []
    for i in range(group):
        c, k = divmod(i, nx)
        taught.append(columns[(place[0] + c) % nc * nx + (place[1] + k) % nx])
        at = dim + c * lane
        rows[-k % nx][:, at : at + lane] = taught[i].astype(bf16)
    for row in rows:
        row[:, :dim] = block[...]
    taught = jnp.concatenate(taught, axis=1)
    top = jnp.max(taught, axis=1, keepdims=True)
    lifted = jnp.exp(taught - top)
    high[...], low[...] = bf16_parts(lifted)
    stats[...] = jnp.concatenate(
        [along_lanes(top), along_lanes(jnp.sum(lifted, axis=1, keepdims=True))]
        + [jnp.zeros((stats.shape[0] - 2, count), f32)],
        axis=0,
    )


def parts_kernel(block, high, low, taught, near, far, sent):
    ny, width, _ = sent.shape
    dim = block.shape[1]
    half = near.shape[0]
    rows = block[...]
    shared = near[...], far[...]
    student = [
        logit_scale * lax.dot_general(rows, p, (((1,), (1,)), ((), ())), preferred_element_type=f32)
        for p in shared
    ]
    top = jnp.maximum(*[jnp.max(v, axis=1, keepdims=True) for v in student])
    total = jnp.zeros_like(top)
    parts = [jnp.zeros(rows.shape, f32) for _ in range(2)]
    for i, p in enumerate(shared):
        lifted = jnp.exp(student[i] - top)
        total += jnp.sum(lifted, axis=1, keepdims=True)
        for piece in bf16_parts(lifted):
            parts[0] += jnp.dot(piece, p, preferred_element_type=f32)
        for piece in (high, low):
            piece = piece[:, i * half : (i + 1) * half]
            parts[1] += jnp.dot(piece, p, preferred_element_type=f32)
    mine = [along_lanes(top), along_lanes(total)]
    spread = jnp.concatenate(mine + [taught[: width - 2]], axis=0)
    for y in range(ny):
        for at in range(2):
            sent[y, :, at * dim : (at + 1) * dim] = parts[at][y * width : (y + 1) * width]
        sent[y, :, 2 * dim :] = spread


vmem = pl.BlockSpec(memory_space=pltpu.VMEM)


def laid_out(got, sizes):
    ny, width, nc, nx, pool, dim = sizes
    count, group = ny * width, nc * nx
    place = jnp.stack([lax.axis_index("core"), lax.axis_index("x")]).astype(jnp.int32)
    lifted = jax.ShapeDtypeStruct((count, group * pool), bf16)
    row = jax.ShapeDtypeStruct((count, dim + nc * pool), bf16)
    block = jax.ShapeDtypeStruct((count, dim), bf16)
    stats = jax.ShapeDtypeStruct((width, count), f32)
    return pl.pallas_call(
        functools.partial(layout_kernel, nc, nx),
        out_shape=(block, lifted, lifted, stats) + (row,) * nx,
        in_specs=[pl.BlockSpec(memory_space=pltpu.SMEM), vmem],
        out_specs=(vmem,) * (4 + nx),
        scratch_shapes=[
            pltpu.VMEM((count * max(group, dim // lane), lane), f32),
            pltpu.VMEM((group, count, pool), f32),
        ],
        compiler_params=pltpu.CompilerParams(vmem_limit_bytes=16 * 2**20),
        cost_estimate=pl.CostEstimate(
            flops=30 * 10**9, bytes_accessed=32 * 2**20, transcendentals=0
        ),
    )(place, got)


def local_parts(block, high, low, stats, near, far, ny):
    count, dim = block.shape
    return pl.pallas_call(
        parts_kernel,
        out_shape=jax.ShapeDtypeStruct((ny, count // ny, 2 * dim + count), f32),
        in_specs=[vmem] * 6,
        out_specs=vmem,
        compiler_params=pltpu.CompilerParams(vmem_limit_bytes=16 * 2**20),
        cost_estimate=pl.CostEstimate(
            flops=10 * count * high.shape[1] * dim,
            bytes_accessed=4 * 2**20,
            transcendentals=count * high.shape[1],
        ),
    )(block, high, low, stats, near.reshape(-1, dim), far.reshape(-1, dim))


def per_device(queries, passages, teacher):
    own, dim = queries.shape
    pool = passages.shape[0]
    ny, nzl, nc, nx, nzh = (lax.axis_size(a) for a in names)
    nz, group = nzh * nzl, nc * nx
    fold = dim // lane

    near = [from_next(passages, "x", k) for k in range(1, nx)]

    tiles = teacher.reshape(own, ny, nzl, nc, nx, nzh, pool)
    tiles = tiles.transpose(5, 2, 1, 0, 3, 4, 6)
    tiles = tiles.reshape(nz, ny * own * group, pool)
    rows = jnp.broadcast_to(queries.reshape(1, own * fold, lane), (nz, own * fold, lane))
    got = exchange(jnp.concatenate([tiles, rows], axis=1), z_axes)
    got, *near = lax.optimization_barrier((got, *near))
    cut = ny * own * group
    tiles = got[:, :cut].reshape(nz, ny, own * group, pool).transpose(1, 0, 2, 3)
    tiles = tiles.reshape(ny, nz * own * group, pool)
    rows = jnp.broadcast_to(got[:, cut:].reshape(1, nz * own * fold, lane), (ny, nz * own * fold, lane))
    sent = jnp.concatenate([tiles, rows], axis=1)
    got = exchange(sent, "y")
    *near, _ = lax.optimization_barrier((*near, sent))
    near = jnp.stack([passages, *near])
    far = from_next(near, "core", 1)
    count = ny * nz * own
    block, high, low, stats, *rows = laid_out(got, (ny, nz * own, nc, nx, pool, dim))
    parts = local_parts(block, high, low, stats, near, far, ny)

    for k in range(1, nx - 1):
        rows[k] = from_next(rows[k], "x", k)

    def pack(parts, stats, n):
        width = parts.shape[0] // n
        extra = -(-stats.size // width)
        extra += -extra % lane
        spread = jnp.pad(stats.reshape(-1, extra), ((0, width - stats.size // extra), (0, 0)))
        spread = jnp.broadcast_to(spread, (n, width, extra))
        return jnp.concatenate([parts.reshape(n, width, 2 * dim), spread], axis=2)

    def unpack(got, place):
        n, width, full = got.shape
        extra = full - 2 * dim
        stats = got[:, : 4 * count // extra, 2 * dim :].reshape(n, 4, count)
        weight_s, top_s, sum_s = combine(stats[:, 0], stats[:, 1], 0)
        weight_t, top_t, sum_t = combine(stats[:, 2], stats[:, 3], 0)
        weight_s = lax.dynamic_slice_in_dim(weight_s, place, width, 1)
        weight_t = lax.dynamic_slice_in_dim(weight_t, place, width, 1)
        part_s = jnp.sum(weight_s[:, :, None] * got[:, :, :dim], axis=0)
        part_t = jnp.sum(weight_t[:, :, None] * got[:, :, dim : 2 * dim], axis=0)
        return part_s, part_t, jnp.stack([top_s, sum_s, top_t, sum_t])

    y_at = lax.axis_index("y") * (nz * own)
    z_at = y_at + lax.axis_index(z_axes) * own
    part_s, part_t, stats = unpack(exchange(parts, "y"), y_at)
    sent = pack(jnp.concatenate([part_s, part_t], axis=1), stats, nz)
    got = exchange(sent, z_axes)
    *rows, _ = lax.optimization_barrier((*rows, sent))
    rows[-1] = from_next(rows[-1], "x", nx - 1)
    kept = jnp.stack([r[:, : dim + pool] for r in rows])
    away = jnp.stack([jnp.concatenate([r[:, :dim], r[:, dim + pool :]], axis=1) for r in rows])
    every_row = jnp.concatenate([kept, from_next(away, "core", 1)]).reshape(group * count, dim + pool)
    all_rows, own_logits = every_row[:, :dim], every_row[:, dim:]

    def lifted(values):
        top = jnp.max(values, axis=0)
        return jnp.exp(values - top), top

    scores, high_s = lifted(
        logit_scale
        * lax.dot_general(passages, all_rows, (((1,), (1,)), ((), ())), preferred_element_type=f32)
    )
    wanted, high_t = lifted(own_logits.T.astype(f32))
    got, scores, wanted, high_s, high_t = lax.optimization_barrier(
        (got, scores, wanted, high_s, high_t)
    )
    part_s, part_t, stats = unpack(got, z_at)
    mine = lax.dynamic_slice_in_dim(stats, z_at, own, 1)
    query_grad = logit_scale * (part_s / mine[1][:, None] - part_t / mine[3][:, None])

    every = exchange(jnp.broadcast_to(stats[None], (group,) + stats.shape), group_axes)
    every = rolled(rolled(every.reshape(nc, nx, 4, count), "x", 1), "core", 0)
    every = every.transpose(2, 0, 1, 3).reshape(4, group * count)
    grad = (logit_scale * jnp.exp(high_s - every[0]) / every[1]) * scores - (
        logit_scale * jnp.exp(high_t - every[2]) / every[3]
    ) * wanted
    passage_grad = split_dot(grad, all_rows, (((1,), (0,)), ((), ())))
    return query_grad, passage_grad


def solution(mesh):
    shape = sizes if mesh.devices.size == 512 else (2,) * 5
    fine = Mesh(mesh.devices.reshape(shape), names)
    placed = P(names, None)
    return jax.shard_map(
        per_device,
        mesh=fine,
        in_specs=(placed, placed, placed),
        out_specs=(placed, placed),
        check_vma=False,
    )
```

```python
import functools

import jax
import jax.numpy as jnp
from jax import lax
from jax.experimental import pallas as pl
from jax.experimental.pallas import tpu as pltpu
from jax.sharding import Mesh
from jax.sharding import PartitionSpec as P

logit_scale = 0.125
names = ("y", "zl", "core", "x", "zh")
sizes = (4, 8, 2, 4, 2)
z_axes = ("zh", "zl")
group_axes = ("core", "x")
lane = 128
f32 = jnp.float32
bf16 = jnp.bfloat16


def exchange(values, axes):
    return lax.all_to_all(values, axes, 0, 0, tiled=True)


def from_next(values, axis, step):
    n = lax.axis_size(axis)
    return lax.ppermute(values, axis, [(i, (i - step) % n) for i in range(n)])


def rolled(values, axis, dim):
    twice = jnp.concatenate([values, values], axis=dim)
    return lax.dynamic_slice_in_dim(twice, lax.axis_index(axis), lax.axis_size(axis), dim)


def split_dot(weights, exact, dims):
    high = lax.reduce_precision(weights, 8, 7)
    low = weights - high
    return lax.dot_general(
        high.astype(bf16), exact, dims, preferred_element_type=f32
    ) + lax.dot_general(low.astype(bf16), exact, dims, preferred_element_type=f32)


def combine(top, total, axis):
    high = jnp.max(top, axis=axis, keepdims=True)
    weight = jnp.exp(top - high)
    return weight, jnp.squeeze(high, axis), jnp.sum(weight * total, axis=axis)


def bf16_parts(values):
    high = values.astype(bf16)
    return high, (values - high.astype(f32)).astype(bf16)


def along_lanes(column):
    n = column.shape[0]
    at_row = lax.broadcasted_iota(jnp.int32, (n, n), 0)
    at_lane = lax.broadcasted_iota(jnp.int32, (n, n), 1)
    return jnp.sum(jnp.where(at_row == at_lane, column, 0.0), axis=0, keepdims=True)


def first_kernel(sizes, queries, teacher, sent):
    ny, nzl, group, nzh, pool = sizes
    for zh in range(nzh):
        for zl in range(nzl):
            to = zh * nzl + zl
            for y in range(ny):
                for i in range(group):
                    at = (((y * nzl + zl) * group + i) * nzh + zh) * pool
                    into = (y * group + i) * pool
                    sent[to, :, into : into + pool] = teacher[:, at : at + pool]
            sent[to, :, ny * group * pool :] = queries[...]


def layout_kernel(nc, nx, place, got, block, high, low, stats, *rows):
    count, dim = block.shape
    group = nc * nx
    block[...] = got[:, group * lane :]
    taught = []
    for i in range(group):
        c, k = divmod(i, nx)
        at = (place[0] + c) % nc * nx + (place[1] + k) % nx
        column = got[:, pl.ds(pl.multiple_of(at * lane, lane), lane)]
        rows[-k % nx][:, dim + c * lane : dim + (c + 1) * lane] = column
        taught.append(column.astype(f32))
    for row in rows:
        row[:, :dim] = block[...]
    taught = jnp.concatenate(taught, axis=1)
    top = jnp.max(taught, axis=1, keepdims=True)
    lifted = jnp.exp(taught - top)
    high[...], low[...] = bf16_parts(lifted)
    stats[...] = jnp.concatenate(
        [along_lanes(top), along_lanes(jnp.sum(lifted, axis=1, keepdims=True))]
        + [jnp.zeros((stats.shape[0] - 2, count), f32)],
        axis=0,
    )


def parts_kernel(block, high, low, taught, near, far, sent):
    ny, width, _ = sent.shape
    count, dim = block.shape
    half = near.shape[0]
    rows = block[...]
    shared = near[...], far[...]
    student = [
        logit_scale * lax.dot_general(rows, p, (((1,), (1,)), ((), ())), preferred_element_type=f32)
        for p in shared
    ]
    top = jnp.maximum(*[jnp.max(v, axis=1, keepdims=True) for v in student])
    total = jnp.zeros_like(top)
    stacked = jnp.zeros((4 * count, dim), f32)
    for i, p in enumerate(shared):
        lifted = jnp.exp(student[i] - top)
        total += jnp.sum(lifted, axis=1, keepdims=True)
        pieces = bf16_parts(lifted) + tuple(v[:, i * half : (i + 1) * half] for v in (high, low))
        stacked += jnp.dot(jnp.concatenate(pieces, axis=0), p, preferred_element_type=f32)
    parts = [
        stacked[at * count : (at + 1) * count] + stacked[(at + 1) * count : (at + 2) * count] for at in (0, 2)
    ]
    mine = [along_lanes(top), along_lanes(total)]
    spread = jnp.concatenate(mine + [taught[: width - 2]], axis=0)
    for y in range(ny):
        for at in range(2):
            sent[y, :, at * dim : (at + 1) * dim] = parts[at][y * width : (y + 1) * width]
        sent[y, :, 2 * dim :] = spread


vmem = pl.BlockSpec(memory_space=pltpu.VMEM)


def first_buffer(queries, teacher, sizes):
    ny, nzl, group, nzh, pool = sizes
    own, dim = queries.shape
    return pl.pallas_call(
        functools.partial(first_kernel, sizes),
        out_shape=jax.ShapeDtypeStruct((nzh * nzl, own, ny * group * pool + dim), bf16),
        in_specs=[vmem] * 2,
        out_specs=vmem,
        compiler_params=pltpu.CompilerParams(vmem_limit_bytes=16 * 2**20),
        cost_estimate=pl.CostEstimate(flops=0, bytes_accessed=2**20, transcendentals=0),
    )(queries, teacher)


def laid_out(got, sizes):
    ny, width, nc, nx, pool, dim = sizes
    count, group = ny * width, nc * nx
    place = jnp.stack([lax.axis_index("core"), lax.axis_index("x")]).astype(jnp.int32)
    lifted = jax.ShapeDtypeStruct((count, group * pool), bf16)
    row = jax.ShapeDtypeStruct((count, dim + nc * pool), bf16)
    block = jax.ShapeDtypeStruct((count, dim), bf16)
    stats = jax.ShapeDtypeStruct((width, count), f32)
    return pl.pallas_call(
        functools.partial(layout_kernel, nc, nx),
        out_shape=(block, lifted, lifted, stats) + (row,) * nx,
        in_specs=[pl.BlockSpec(memory_space=pltpu.SMEM), vmem],
        out_specs=(vmem,) * (4 + nx),
        compiler_params=pltpu.CompilerParams(vmem_limit_bytes=16 * 2**20),
        cost_estimate=pl.CostEstimate(
            flops=30 * 10**9, bytes_accessed=32 * 2**20, transcendentals=0
        ),
    )(place, got)


def local_parts(block, high, low, stats, near, far, ny):
    count, dim = block.shape
    return pl.pallas_call(
        parts_kernel,
        out_shape=jax.ShapeDtypeStruct((ny, count // ny, 2 * dim + count), f32),
        in_specs=[vmem] * 6,
        out_specs=vmem,
        compiler_params=pltpu.CompilerParams(vmem_limit_bytes=16 * 2**20),
        cost_estimate=pl.CostEstimate(
            flops=10 * count * high.shape[1] * dim,
            bytes_accessed=4 * 2**20,
            transcendentals=count * high.shape[1],
        ),
    )(block, high, low, stats, near.reshape(-1, dim), far.reshape(-1, dim))


def per_device(queries, passages, teacher):
    own, dim = queries.shape
    pool = passages.shape[0]
    ny, nzl, nc, nx, nzh = (lax.axis_size(a) for a in names)
    nz, group = nzh * nzl, nc * nx

    near = [from_next(passages, "x", k) for k in range(1, nx)]

    got = exchange(first_buffer(queries, teacher, (ny, nzl, group, nzh, pool)), z_axes)
    got, *near = lax.optimization_barrier((got, *near))
    width, count = nz * own, ny * nz * own
    got = got.reshape(width, -1)
    tiles = [got[:, i * group * pool : (i + 1) * group * pool] for i in range(ny)]
    sent = jnp.stack([jnp.concatenate([t, got[:, ny * group * pool :]], axis=1) for t in tiles])
    got = exchange(sent, "y")
    *near, _ = lax.optimization_barrier((*near, sent))
    near = jnp.stack([passages, *near])
    far = from_next(near, "core", 1)
    block, high, low, stats, *rows = laid_out(got.reshape(count, -1), (ny, width, nc, nx, pool, dim))
    parts = local_parts(block, high, low, stats, near, far, ny)

    for k in range(1, nx - 1):
        rows[k] = from_next(rows[k], "x", k)

    def pack(parts, stats, n):
        width = parts.shape[0] // n
        extra = -(-stats.size // width)
        extra += -extra % lane
        spread = jnp.pad(stats.reshape(-1, extra), ((0, width - stats.size // extra), (0, 0)))
        spread = jnp.broadcast_to(spread, (n, width, extra))
        return jnp.concatenate([parts.reshape(n, width, 2 * dim), spread], axis=2)

    def unpack(got, place):
        n, width, full = got.shape
        extra = full - 2 * dim
        stats = got[:, : 4 * count // extra, 2 * dim :].reshape(n, 4, count)
        weight_s, top_s, sum_s = combine(stats[:, 0], stats[:, 1], 0)
        weight_t, top_t, sum_t = combine(stats[:, 2], stats[:, 3], 0)
        weight_s = lax.dynamic_slice_in_dim(weight_s, place, width, 1)
        weight_t = lax.dynamic_slice_in_dim(weight_t, place, width, 1)
        part_s = jnp.sum(weight_s[:, :, None] * got[:, :, :dim], axis=0)
        part_t = jnp.sum(weight_t[:, :, None] * got[:, :, dim : 2 * dim], axis=0)
        return part_s, part_t, jnp.stack([top_s, sum_s, top_t, sum_t])

    y_at = lax.axis_index("y") * (nz * own)
    z_at = y_at + lax.axis_index(z_axes) * own
    part_s, part_t, stats = unpack(exchange(parts, "y"), y_at)
    sent = pack(jnp.concatenate([part_s, part_t], axis=1), stats, nz)
    got = exchange(sent, z_axes)
    *rows, _ = lax.optimization_barrier((*rows, sent))
    rows[-1] = from_next(rows[-1], "x", nx - 1)
    kept = jnp.stack([r[:, : dim + pool] for r in rows])
    away = jnp.stack([jnp.concatenate([r[:, :dim], r[:, dim + pool :]], axis=1) for r in rows])
    every_row = jnp.concatenate([kept, from_next(away, "core", 1)]).reshape(group * count, dim + pool)
    all_rows, own_logits = every_row[:, :dim], every_row[:, dim:]

    def lifted(values):
        top = jnp.max(values, axis=0)
        return jnp.exp(values - top), top

    scores, high_s = lifted(
        logit_scale
        * lax.dot_general(passages, all_rows, (((1,), (1,)), ((), ())), preferred_element_type=f32)
    )
    wanted, high_t = lifted(own_logits.T.astype(f32))
    got, scores, wanted, high_s, high_t = lax.optimization_barrier(
        (got, scores, wanted, high_s, high_t)
    )
    part_s, part_t, stats = unpack(got, z_at)
    mine = lax.dynamic_slice_in_dim(stats, z_at, own, 1)
    query_grad = logit_scale * (part_s / mine[1][:, None] - part_t / mine[3][:, None])

    every = exchange(jnp.broadcast_to(stats[None], (group,) + stats.shape), group_axes)
    every = rolled(rolled(every.reshape(nc, nx, 4, count), "x", 1), "core", 0)
    every = every.transpose(2, 0, 1, 3).reshape(4, group * count)
    grad = (logit_scale * jnp.exp(high_s - every[0]) / every[1]) * scores - (
        logit_scale * jnp.exp(high_t - every[2]) / every[3]
    ) * wanted
    passage_grad = split_dot(grad, all_rows, (((1,), (0,)), ((), ())))
    return query_grad, passage_grad


def solution(mesh):
    shape = sizes if mesh.devices.size == 512 else (2,) * 5
    fine = Mesh(mesh.devices.reshape(shape), names)
    placed = P(names, None)
    return jax.shard_map(
        per_device,
        mesh=fine,
        in_specs=(placed, placed, placed),
        out_specs=(placed, placed),
        check_vma=False,
    )
```

```python
import functools

import jax
import jax.numpy as jnp
from jax import lax
from jax.experimental import pallas as pl
from jax.experimental.pallas import tpu as pltpu
from jax.sharding import Mesh
from jax.sharding import PartitionSpec as P

logit_scale = 0.125
names = ("y", "zl", "core", "x", "zh")
sizes = (4, 8, 2, 4, 2)
z_axes = ("zh", "zl")
group_axes = ("core", "x")
lane = 128
f32 = jnp.float32
bf16 = jnp.bfloat16


def exchange(values, axes):
    return lax.all_to_all(values, axes, 0, 0, tiled=True)


def from_next(values, axis, step):
    n = lax.axis_size(axis)
    return lax.ppermute(values, axis, [(i, (i - step) % n) for i in range(n)])


def bf16_parts(values):
    high = values.astype(bf16)
    return high, (values - high.astype(f32)).astype(bf16)


def along_lanes(column):
    n = column.shape[0]
    at_row = lax.broadcasted_iota(jnp.int32, (n, n), 0)
    at_lane = lax.broadcasted_iota(jnp.int32, (n, n), 1)
    return jnp.sum(jnp.where(at_row == at_lane, column, 0.0), axis=0, keepdims=True)


def first_kernel(sizes, queries_in, teacher_in, sent, queries, teacher, sems):
    ny, nzl, group, nzh, pool = sizes
    copies = [
        pltpu.make_async_copy(teacher_in, teacher, sems.at[0]),
        pltpu.make_async_copy(queries_in, queries, sems.at[1]),
    ]
    for copy in copies:
        copy.start()
    for copy in copies:
        copy.wait()
    for zh in range(nzh):
        for zl in range(nzl):
            to = zh * nzl + zl
            for y in range(ny):
                for i in range(group):
                    at = (((y * nzl + zl) * group + i) * nzh + zh) * pool
                    into = (y * group + i) * pool
                    sent[to, :, into : into + pool] = teacher[:, at : at + pool]
            sent[to, :, ny * group * pool :] = queries[...]


def layout_kernel(nc, nx, place, got, block, high, low, stats, *rows):
    count, dim = block.shape
    group = nc * nx
    block[...] = got[:, group * lane :]
    taught = []
    for i in range(group):
        c, k = divmod(i, nx)
        at = (place[0] + c) % nc * nx + (place[1] + k) % nx
        column = got[:, pl.ds(pl.multiple_of(at * lane, lane), lane)]
        rows[-k % nx][:, dim + c * lane : dim + (c + 1) * lane] = column
        taught.append(column.astype(f32))
    for row in rows:
        row[:, :dim] = block[...]
    taught = jnp.concatenate(taught, axis=1)
    top = jnp.max(taught, axis=1, keepdims=True)
    lifted = jnp.exp(taught - top)
    high[...], low[...] = bf16_parts(lifted)
    stats[...] = jnp.concatenate(
        [along_lanes(top), along_lanes(jnp.sum(lifted, axis=1, keepdims=True))]
        + [jnp.zeros((stats.shape[0] - 2, count), f32)],
        axis=0,
    )


def parts_kernel(block, high, low, taught, near, far, sent):
    ny, width, _ = sent.shape
    count, dim = block.shape
    half = near.shape[0]
    rows = block[...]
    shared = near[...], far[...]
    student = [
        logit_scale * lax.dot_general(rows, p, (((1,), (1,)), ((), ())), preferred_element_type=f32)
        for p in shared
    ]
    top = jnp.maximum(*[jnp.max(v, axis=1, keepdims=True) for v in student])
    total = jnp.zeros_like(top)
    stacked = jnp.zeros((4 * count, dim), f32)
    for i, p in enumerate(shared):
        lifted = jnp.exp(student[i] - top)
        total += jnp.sum(lifted, axis=1, keepdims=True)
        pieces = bf16_parts(lifted) + tuple(v[:, i * half : (i + 1) * half] for v in (high, low))
        stacked += jnp.dot(jnp.concatenate(pieces, axis=0), p, preferred_element_type=f32)
    parts = [
        stacked[at * count : (at + 1) * count] + stacked[(at + 1) * count : (at + 2) * count] for at in (0, 2)
    ]
    mine = [along_lanes(top), along_lanes(total)]
    spread = jnp.concatenate(mine + [taught[: width - 2]], axis=0)
    for y in range(ny):
        for at in range(2):
            sent[y, :, at * dim : (at + 1) * dim] = parts[at][y * width : (y + 1) * width]
        sent[y, :, 2 * dim :] = spread


def merged(pairs):
    high = functools.reduce(jnp.maximum, [top for top, _ in pairs])
    weights = [jnp.exp(top - high) for top, _ in pairs]
    total = functools.reduce(jnp.add, [w * t for w, (_, t) in zip(weights, pairs)])
    return weights, high, total


def stats_place(own, count, i):
    rows = min(own, 4)
    row, at = divmod(i, 4 // rows)
    return row, at * count


def middle_kernel(place, got, sent):
    nz, own, _ = sent.shape
    ny, width, full = got.shape
    count = ny * width
    dim = (full - count) // 2
    at_lane = lax.broadcasted_iota(jnp.int32, (width, count), 1)
    at_row = lax.broadcasted_iota(jnp.int32, (width, count), 0)
    mine = at_lane == at_row + place[0] * width
    stats = []
    for at in range(2):
        pairs = [
            tuple(got[y, 2 * at + i : 2 * at + i + 1, 2 * dim :] for i in range(2)) for y in range(ny)
        ]
        weights, high, total = merged(pairs)
        stats += [high, total]
        part = jnp.zeros((width, dim), f32)
        for y, weight in enumerate(weights):
            column = jnp.sum(jnp.where(mine, weight, 0.0), axis=1, keepdims=True)
            part += column * got[y, :, at * dim : (at + 1) * dim]
        for z in range(nz):
            sent[z, :, at * dim : (at + 1) * dim] = part[z * own : (z + 1) * own]
    for i, values in enumerate(stats):
        row, at = stats_place(own, count, i)
        for z in range(nz):
            sent[z, row : row + 1, 2 * dim + at : 2 * dim + at + count] = values


def all_pairs(got, dim, count, kind):
    nz, own, _ = got.shape
    pairs = []
    for z in range(nz):
        pair = []
        for i in (2 * kind, 2 * kind + 1):
            row, at = stats_place(own, count, i)
            pair.append(got[z, row : row + 1, 2 * dim + at : 2 * dim + at + count])
        pairs.append(pair)
    return pairs


def after_kernel(dim, got, sent):
    group, _, count = sent.shape
    stats = [v for kind in range(2) for v in merged(all_pairs(got, dim, count, kind))[1:]]
    stats = jnp.concatenate(stats, axis=0)
    for i in range(group):
        sent[i] = stats


def query_kernel(count, place, got, grads):
    own, dim = grads.shape
    at_lane = lax.broadcasted_iota(jnp.int32, (own, count), 1)
    at_row = lax.broadcasted_iota(jnp.int32, (own, count), 0)
    mine = at_lane == at_row + place[0]

    def column(values):
        return jnp.sum(jnp.where(mine, values, 0.0), axis=1, keepdims=True)

    parts = []
    for kind in range(2):
        weights, _, total = merged(all_pairs(got, dim, count, kind))
        part = jnp.zeros((own, dim), f32)
        for z, weight in enumerate(weights):
            part += column(weight) * got[z, :, kind * dim : (kind + 1) * dim]
        parts.append(part / column(total))
    grads[...] = logit_scale * (parts[0] - parts[1])


def last_kernel(blocks, nc, nx, place, got, *rest):
    *sets, grads = rest
    count = got.shape[2]
    dim = grads.shape[1]
    total = jnp.zeros((2 * grads.shape[0], dim), f32)
    for j, block in enumerate(blocks):
        scores, wanted, high_s, high_t, rows = sets[5 * j : 5 * j + 5]
        pieces = []
        for i, (c, k) in enumerate(block):
            of = (place[0] + c) % nc * nx + (place[1] + k) % nx
            at = slice(i * count, (i + 1) * count)
            stats = got[of]
            weight_s = logit_scale * jnp.exp(high_s[:, at] - stats[0:1]) / stats[1:2]
            weight_t = logit_scale * jnp.exp(high_t[:, at] - stats[2:3]) / stats[3:4]
            grad = weight_s * scores[:, at] - weight_t * wanted[:, at]
            pieces.append(jnp.concatenate(bf16_parts(grad), axis=0))
        total += jnp.dot(
            jnp.concatenate(pieces, axis=1), rows[:, :dim], preferred_element_type=f32
        )
    grads[...] = total[: grads.shape[0]] + total[grads.shape[0] :]


vmem = pl.BlockSpec(memory_space=pltpu.VMEM)


def first_buffer(queries, teacher, sizes):
    ny, nzl, group, nzh, pool = sizes
    own, dim = queries.shape
    return pl.pallas_call(
        functools.partial(first_kernel, sizes),
        out_shape=jax.ShapeDtypeStruct((nzh * nzl, own, ny * group * pool + dim), bf16),
        in_specs=[pl.BlockSpec(memory_space=pltpu.HBM)] * 2,
        out_specs=vmem,
        scratch_shapes=[
            pltpu.VMEM(queries.shape, bf16),
            pltpu.VMEM(teacher.shape, bf16),
            pltpu.SemaphoreType.DMA((2,)),
        ],
        compiler_params=pltpu.CompilerParams(vmem_limit_bytes=60 * 2**20),
        cost_estimate=pl.CostEstimate(flops=0, bytes_accessed=2**20, transcendentals=0),
    )(queries, teacher)


def place_of():
    return jnp.stack([lax.axis_index("core"), lax.axis_index("x")]).astype(jnp.int32)


def laid_out(got, sizes):
    ny, width, nc, nx, pool, dim = sizes
    count, group = ny * width, nc * nx
    place = place_of()
    lifted = jax.ShapeDtypeStruct((count, group * pool), bf16)
    row = jax.ShapeDtypeStruct((count, dim + nc * pool), bf16)
    block = jax.ShapeDtypeStruct((count, dim), bf16)
    stats = jax.ShapeDtypeStruct((width, count), f32)
    return pl.pallas_call(
        functools.partial(layout_kernel, nc, nx),
        out_shape=(block, lifted, lifted, stats) + (row,) * nx,
        in_specs=[pl.BlockSpec(memory_space=pltpu.SMEM), vmem],
        out_specs=(vmem,) * (4 + nx),
        compiler_params=pltpu.CompilerParams(vmem_limit_bytes=16 * 2**20),
        cost_estimate=pl.CostEstimate(
            flops=30 * 10**9, bytes_accessed=32 * 2**20, transcendentals=0
        ),
    )(place, got)


def local_parts(block, high, low, stats, near, far, ny):
    count, dim = block.shape
    return pl.pallas_call(
        parts_kernel,
        out_shape=jax.ShapeDtypeStruct((ny, count // ny, 2 * dim + count), f32),
        in_specs=[vmem] * 6,
        out_specs=vmem,
        compiler_params=pltpu.CompilerParams(vmem_limit_bytes=16 * 2**20),
        cost_estimate=pl.CostEstimate(
            flops=10 * count * high.shape[1] * dim,
            bytes_accessed=4 * 2**20,
            transcendentals=count * high.shape[1],
        ),
    )(block, high, low, stats, near.reshape(-1, dim), far.reshape(-1, dim))


def simple_call(kernel, out, scalars, arrays, flops=0):
    size = sum(v.size * v.dtype.itemsize for v in arrays) + 4 * out.size
    smem = pl.BlockSpec(memory_space=pltpu.SMEM)
    return pl.pallas_call(
        kernel,
        out_shape=out,
        in_specs=[smem] * len(scalars) + [vmem] * len(arrays),
        out_specs=vmem,
        compiler_params=pltpu.CompilerParams(vmem_limit_bytes=16 * 2**20),
        cost_estimate=pl.CostEstimate(flops=flops, bytes_accessed=size, transcendentals=0),
    )(*scalars, *arrays)


def per_device(queries, passages, teacher):
    own, dim = queries.shape
    pool = passages.shape[0]
    ny, nzl, nc, nx, nzh = (lax.axis_size(a) for a in names)
    nz, group = nzh * nzl, nc * nx

    near = [from_next(passages, "x", k) for k in range(1, nx)]

    got = exchange(first_buffer(queries, teacher, (ny, nzl, group, nzh, pool)), z_axes)
    got, *near = lax.optimization_barrier((got, *near))
    width, count = nz * own, ny * nz * own
    got = got.reshape(width, -1)
    tiles = [got[:, i * group * pool : (i + 1) * group * pool] for i in range(ny)]
    sent = jnp.stack([jnp.concatenate([t, got[:, ny * group * pool :]], axis=1) for t in tiles])
    got = exchange(sent, "y")
    *near, _ = lax.optimization_barrier((*near, sent))
    near = jnp.stack([passages, *near])
    far = from_next(near, "core", 1)
    block, high, low, stats, *rows = laid_out(got.reshape(count, -1), (ny, width, nc, nx, pool, dim))
    parts = local_parts(block, high, low, stats, near, far, ny)

    for k in range(1, nx - 1):
        rows[k] = from_next(rows[k], "x", k)

    z_at = lax.axis_index("y") * width + lax.axis_index(z_axes) * own
    extra = 4 // min(own, 4) * count
    sent = simple_call(
        middle_kernel,
        jax.ShapeDtypeStruct((nz, own, 2 * dim + extra), f32),
        [lax.axis_index("y").astype(jnp.int32)[None]],
        [exchange(parts, "y")],
    )
    got = exchange(sent, z_axes)
    *rows, _ = lax.optimization_barrier((*rows, sent))
    rows[-1] = from_next(rows[-1], "x", nx - 1)

    kept = jnp.stack([r[:, : dim + pool] for r in rows])
    away = jnp.stack([jnp.concatenate([r[:, :dim], r[:, dim + pool :]], axis=1) for r in rows])
    every_row = jnp.concatenate([kept, from_next(away, "core", 1)]).reshape(group * count, dim + pool)
    row_sets = [every_row]
    blocks = [[(c, k) for c in range(nc) for k in range(nx)]]

    def lifted(values):
        top = jnp.max(values, axis=0)
        return jnp.exp(values - top), top

    scores, high_s = lifted(
        logit_scale
        * lax.dot_general(
            passages, every_row[:, :dim], (((1,), (1,)), ((), ())), preferred_element_type=f32
        )
    )
    wanted, high_t = lifted(every_row[:, dim:].T.astype(f32))
    sets = [scores, wanted, high_s, high_t]
    got, *sets = lax.optimization_barrier((got, *sets))
    sets = [*sets[:2], sets[2][None], sets[3][None], every_row]
    every = simple_call(
        functools.partial(after_kernel, dim), jax.ShapeDtypeStruct((group, 4, count), f32), [], [got]
    )
    got, _ = lax.optimization_barrier((got, every))
    every = exchange(every, group_axes)
    query_grad = simple_call(
        functools.partial(query_kernel, count),
        jax.ShapeDtypeStruct((own, dim), f32),
        [z_at.astype(jnp.int32)[None]],
        [got],
    )

    passage_grad = simple_call(
        functools.partial(last_kernel, blocks, nc, nx),
        jax.ShapeDtypeStruct((pool, dim), f32),
        [place_of()],
        [every, *sets],
        flops=4 * pool * group * count * dim,
    )
    return query_grad, passage_grad


def solution(mesh):
    shape = sizes if mesh.devices.size == 512 else (2,) * 5
    fine = Mesh(mesh.devices.reshape(shape), names)
    placed = P(names, None)
    return jax.shard_map(
        per_device,
        mesh=fine,
        in_specs=(placed, placed, placed),
        out_specs=(placed, placed),
        check_vma=False,
    )
```

```python
import functools

import jax
import jax.numpy as jnp
from jax import lax
from jax.experimental import pallas as pl
from jax.experimental.pallas import tpu as pltpu
from jax.sharding import Mesh
from jax.sharding import PartitionSpec as P

logit_scale = 0.125
names = ("y", "zl", "core", "x", "zh")
sizes = (4, 8, 2, 4, 2)
z_axes = ("zh", "zl")
lane = 128
f32 = jnp.float32
bf16 = jnp.bfloat16


def exchange(values, axes):
    return lax.all_to_all(values, axes, 0, 0, tiled=True)


def from_next(values, axis, step):
    n = lax.axis_size(axis)
    return lax.ppermute(values, axis, [(i, (i - step) % n) for i in range(n)])


def bf16_parts(values):
    high = values.astype(bf16)
    return high, (values - high.astype(f32)).astype(bf16)


def along_lanes(column):
    n = column.shape[0]
    at_row = lax.broadcasted_iota(jnp.int32, (n, n), 0)
    at_lane = lax.broadcasted_iota(jnp.int32, (n, n), 1)
    return jnp.sum(jnp.where(at_row == at_lane, column, 0.0), axis=0, keepdims=True)


def first_kernel(sizes, queries_in, teacher_in, sent, queries, teacher, sems):
    ny, nzl, group, nzh, pool = sizes
    copies = [
        pltpu.make_async_copy(teacher_in, teacher, sems.at[0]),
        pltpu.make_async_copy(queries_in, queries, sems.at[1]),
    ]
    for copy in copies:
        copy.start()
    for copy in copies:
        copy.wait()
    for zh in range(nzh):
        for zl in range(nzl):
            to = zh * nzl + zl
            for y in range(ny):
                for i in range(group):
                    at = (((y * nzl + zl) * group + i) * nzh + zh) * pool
                    into = (y * group + i) * pool
                    sent[to, :, into : into + pool] = teacher[:, at : at + pool]
            sent[to, :, ny * group * pool :] = queries[...]


def layout_kernel(nc, nx, place, got, block, high, low, stats, *rows):
    count, dim = block.shape
    group = nc * nx
    block[...] = got[:, group * lane :]
    taught = []
    for i in range(group):
        c, k = divmod(i, nx)
        at = (place[0] + c) % nc * nx + (place[1] + k) % nx
        column = got[:, pl.ds(pl.multiple_of(at * lane, lane), lane)]
        rows[-k % nx][:, dim + c * lane : dim + (c + 1) * lane] = column
        taught.append(column.astype(f32))
    for row in rows:
        row[:, :dim] = block[...]
    taught = jnp.concatenate(taught, axis=1)
    top = jnp.max(taught, axis=1, keepdims=True)
    lifted = jnp.exp(taught - top)
    high[...], low[...] = bf16_parts(lifted)
    stats[...] = jnp.concatenate(
        [along_lanes(top), along_lanes(jnp.sum(lifted, axis=1, keepdims=True))]
        + [jnp.zeros((stats.shape[0] - 2, count), f32)],
        axis=0,
    )


def parts_kernel(block, high, low, taught, near, far, sent):
    ny, width, _ = sent.shape
    count, dim = block.shape
    half = near.shape[0]
    rows = block[...]
    shared = near[...], far[...]
    student = [
        logit_scale * lax.dot_general(rows, p, (((1,), (1,)), ((), ())), preferred_element_type=f32)
        for p in shared
    ]
    top = jnp.maximum(*[jnp.max(v, axis=1, keepdims=True) for v in student])
    total = jnp.zeros_like(top)
    stacked = jnp.zeros((4 * count, dim), f32)
    for i, p in enumerate(shared):
        lifted = jnp.exp(student[i] - top)
        total += jnp.sum(lifted, axis=1, keepdims=True)
        pieces = bf16_parts(lifted) + tuple(v[:, i * half : (i + 1) * half] for v in (high, low))
        stacked += jnp.dot(jnp.concatenate(pieces, axis=0), p, preferred_element_type=f32)
    parts = [
        stacked[at * count : (at + 1) * count] + stacked[(at + 1) * count : (at + 2) * count] for at in (0, 2)
    ]
    mine = [along_lanes(top), along_lanes(total)]
    spread = jnp.concatenate(mine + [taught[: width - 2]], axis=0)
    for y in range(ny):
        for at in range(2):
            sent[y, :, at * dim : (at + 1) * dim] = parts[at][y * width : (y + 1) * width]
        sent[y, :, 2 * dim :] = spread


def merged(pairs):
    high = functools.reduce(jnp.maximum, [top for top, _ in pairs])
    weights = [jnp.exp(top - high) for top, _ in pairs]
    total = functools.reduce(jnp.add, [w * t for w, (_, t) in zip(weights, pairs)])
    return weights, high, total


def stats_place(own, count, i):
    rows = min(own, 4)
    row, at = divmod(i, 4 // rows)
    return row, at * count


def middle_kernel(place, got, sent):
    nz, own, _ = sent.shape
    ny, width, full = got.shape
    count = ny * width
    dim = (full - count) // 2
    at_lane = lax.broadcasted_iota(jnp.int32, (width, count), 1)
    at_row = lax.broadcasted_iota(jnp.int32, (width, count), 0)
    mine = at_lane == at_row + place[0] * width
    stats = []
    for at in range(2):
        pairs = [
            tuple(got[y, 2 * at + i : 2 * at + i + 1, 2 * dim :] for i in range(2)) for y in range(ny)
        ]
        weights, high, total = merged(pairs)
        stats += [high, total]
        part = jnp.zeros((width, dim), f32)
        for y, weight in enumerate(weights):
            column = jnp.sum(jnp.where(mine, weight, 0.0), axis=1, keepdims=True)
            part += column * got[y, :, at * dim : (at + 1) * dim]
        for z in range(nz):
            sent[z, :, at * dim : (at + 1) * dim] = part[z * own : (z + 1) * own]
    for i, values in enumerate(stats):
        row, at = stats_place(own, count, i)
        for z in range(nz):
            sent[z, row : row + 1, 2 * dim + at : 2 * dim + at + count] = values


def all_pairs(got, dim, count, kind):
    nz, own, _ = got.shape
    pairs = []
    for z in range(nz):
        pair = []
        for i in (2 * kind, 2 * kind + 1):
            row, at = stats_place(own, count, i)
            pair.append(got[z, row : row + 1, 2 * dim + at : 2 * dim + at + count])
        pairs.append(pair)
    return pairs


def after_kernel(dim, got, sent):
    group, _, count = sent.shape
    stats = [v for kind in range(2) for v in merged(all_pairs(got, dim, count, kind))[1:]]
    stats = jnp.concatenate(stats, axis=0)
    for i in range(group):
        sent[i] = stats


def query_kernel(count, place, got, grads):
    own, dim = grads.shape
    at_lane = lax.broadcasted_iota(jnp.int32, (own, count), 1)
    at_row = lax.broadcasted_iota(jnp.int32, (own, count), 0)
    mine = at_lane == at_row + place[0]

    def column(values):
        return jnp.sum(jnp.where(mine, values, 0.0), axis=1, keepdims=True)

    parts = []
    for kind in range(2):
        weights, _, total = merged(all_pairs(got, dim, count, kind))
        part = jnp.zeros((own, dim), f32)
        for z, weight in enumerate(weights):
            part += column(weight) * got[z, :, kind * dim : (kind + 1) * dim]
        parts.append(part / column(total))
    grads[...] = logit_scale * (parts[0] - parts[1])


def own_kernel(passages, rows, scores, wanted, tops):
    pool, dim = passages.shape
    own = passages[...]
    for at in range(0, rows.shape[0], 2 * lane):
        at = slice(at, at + 2 * lane)
        student = logit_scale * lax.dot_general(
            own, rows[at, :dim], (((1,), (1,)), ((), ())), preferred_element_type=f32
        )
        taught = rows[at, dim : dim + pool].astype(f32).T
        for values, out, which in ((student, scores, 0), (taught, wanted, 1)):
            top = jnp.max(values, axis=0, keepdims=True)
            out[:, at] = jnp.exp(values - top)
            tops[which : which + 1, at] = top


def last_kernel(nc, nx, place, got, scores, wanted, tops, rows, grads):
    count = got.shape[2]
    pool, dim = grads.shape
    total = jnp.zeros((2 * pool, dim), f32)
    for i in range(0, nc * nx, 2):
        pieces = []
        for j in (i, i + 1):
            c, k = divmod(j, nx)
            at = slice(j * count, (j + 1) * count)
            stats = got[(place[1] + k) % nx * nc + (place[0] + c) % nc]
            weight_s = logit_scale * jnp.exp(tops[0:1, at] - stats[0:1]) / stats[1:2]
            weight_t = logit_scale * jnp.exp(tops[1:2, at] - stats[2:3]) / stats[3:4]
            grad = weight_s * scores[:, at] - weight_t * wanted[:, at]
            pieces.append(jnp.concatenate(bf16_parts(grad), axis=0))
        total += jnp.dot(
            jnp.concatenate(pieces, axis=1),
            rows[i * count : (i + 2) * count, :dim],
            preferred_element_type=f32,
        )
    grads[...] = total[:pool] + total[pool:]


vmem = pl.BlockSpec(memory_space=pltpu.VMEM)


def first_buffer(queries, teacher, sizes):
    ny, nzl, group, nzh, pool = sizes
    own, dim = queries.shape
    return pl.pallas_call(
        functools.partial(first_kernel, sizes),
        out_shape=jax.ShapeDtypeStruct((nzh * nzl, own, ny * group * pool + dim), bf16),
        in_specs=[pl.BlockSpec(memory_space=pltpu.HBM)] * 2,
        out_specs=vmem,
        scratch_shapes=[
            pltpu.VMEM(queries.shape, bf16),
            pltpu.VMEM(teacher.shape, bf16),
            pltpu.SemaphoreType.DMA((2,)),
        ],
        compiler_params=pltpu.CompilerParams(vmem_limit_bytes=60 * 2**20),
        cost_estimate=pl.CostEstimate(flops=0, bytes_accessed=2**20, transcendentals=0),
    )(queries, teacher)


def place_of():
    return jnp.stack([lax.axis_index("core"), lax.axis_index("x")]).astype(jnp.int32)


def laid_out(got, sizes):
    ny, width, nc, nx, pool, dim = sizes
    count, group = ny * width, nc * nx
    place = place_of()
    lifted = jax.ShapeDtypeStruct((count, group * pool), bf16)
    row = jax.ShapeDtypeStruct((count, dim + nc * pool), bf16)
    block = jax.ShapeDtypeStruct((count, dim), bf16)
    stats = jax.ShapeDtypeStruct((width, count), f32)
    return pl.pallas_call(
        functools.partial(layout_kernel, nc, nx),
        out_shape=(block, lifted, lifted, stats) + (row,) * nx,
        in_specs=[pl.BlockSpec(memory_space=pltpu.SMEM), vmem],
        out_specs=(vmem,) * (4 + nx),
        compiler_params=pltpu.CompilerParams(vmem_limit_bytes=16 * 2**20),
        cost_estimate=pl.CostEstimate(
            flops=30 * 10**9, bytes_accessed=32 * 2**20, transcendentals=0
        ),
    )(place, got)


def local_parts(block, high, low, stats, near, far, ny):
    count, dim = block.shape
    return pl.pallas_call(
        parts_kernel,
        out_shape=jax.ShapeDtypeStruct((ny, count // ny, 2 * dim + count), f32),
        in_specs=[vmem] * 6,
        out_specs=vmem,
        compiler_params=pltpu.CompilerParams(vmem_limit_bytes=16 * 2**20),
        cost_estimate=pl.CostEstimate(
            flops=10 * count * high.shape[1] * dim,
            bytes_accessed=4 * 2**20,
            transcendentals=count * high.shape[1],
        ),
    )(block, high, low, stats, near.reshape(-1, dim), far.reshape(-1, dim))


def simple_call(kernel, out, scalars, arrays, flops=0):
    smem = pl.BlockSpec(memory_space=pltpu.SMEM)
    return pl.pallas_call(
        kernel,
        out_shape=out,
        in_specs=[smem] * len(scalars) + [vmem] * len(arrays),
        out_specs=(vmem,) * len(out) if isinstance(out, tuple) else vmem,
        compiler_params=pltpu.CompilerParams(vmem_limit_bytes=16 * 2**20),
        cost_estimate=pl.CostEstimate(flops=flops, bytes_accessed=2**16, transcendentals=0),
    )(*scalars, *arrays)


def per_device(queries, passages, teacher):
    own, dim = queries.shape
    pool = passages.shape[0]
    ny, nzl, nc, nx, nzh = (lax.axis_size(a) for a in names)
    nz, group = nzh * nzl, nc * nx

    near = [from_next(passages, "x", k) for k in range(1, nx)]

    got = exchange(first_buffer(queries, teacher, (ny, nzl, group, nzh, pool)), z_axes)
    got, *near = lax.optimization_barrier((got, *near))
    width, count = nz * own, ny * nz * own
    got = got.reshape(width, -1)
    tiles = [got[:, i * group * pool : (i + 1) * group * pool] for i in range(ny)]
    sent = jnp.stack([jnp.concatenate([t, got[:, ny * group * pool :]], axis=1) for t in tiles])
    got = exchange(sent, "y")
    *near, _ = lax.optimization_barrier((*near, sent))
    near = jnp.stack([passages, *near])
    far = from_next(near, "core", 1)
    block, high, low, stats, *rows = laid_out(got.reshape(count, -1), (ny, width, nc, nx, pool, dim))
    parts = local_parts(block, high, low, stats, near, far, ny)

    for k in range(1, nx - 1):
        rows[k] = from_next(rows[k], "x", k)

    z_at = lax.axis_index("y") * width + lax.axis_index(z_axes) * own
    extra = 4 // min(own, 4) * count
    sent = simple_call(
        middle_kernel,
        jax.ShapeDtypeStruct((nz, own, 2 * dim + extra), f32),
        [lax.axis_index("y").astype(jnp.int32)[None]],
        [exchange(parts, "y")],
    )
    got = exchange(sent, z_axes)
    *rows, _ = lax.optimization_barrier((*rows, sent))
    rows[-1] = from_next(rows[-1], "x", nx - 1)

    kept = jnp.stack([r[:, : dim + pool] for r in rows])
    away = jnp.stack([jnp.concatenate([r[:, :dim], r[:, dim + pool :]], axis=1) for r in rows])
    every_row = jnp.concatenate([kept, from_next(away, "core", 1)]).reshape(group * count, dim + pool)

    lifted = jax.ShapeDtypeStruct((pool, group * count), f32)
    tops = jax.ShapeDtypeStruct((2, group * count), f32)
    sets = simple_call(own_kernel, (lifted, lifted, tops), [], [passages, every_row], flops=2 * pool * group * count * dim)
    got, *sets = lax.optimization_barrier((got, *sets))
    every = simple_call(
        functools.partial(after_kernel, dim), jax.ShapeDtypeStruct((group, 4, count), f32), [], [got]
    )
    got, _ = lax.optimization_barrier((got, every))
    every = exchange(every, ("x", "core"))
    query_grad = simple_call(
        functools.partial(query_kernel, count),
        jax.ShapeDtypeStruct((own, dim), f32),
        [z_at.astype(jnp.int32)[None]],
        [got],
    )

    passage_grad = simple_call(
        functools.partial(last_kernel, nc, nx),
        jax.ShapeDtypeStruct((pool, dim), f32),
        [place_of()],
        [every, *sets, every_row],
    )
    return query_grad, passage_grad


def solution(mesh):
    shape = sizes if mesh.devices.size == 512 else (2,) * 5
    fine = Mesh(mesh.devices.reshape(shape), names)
    placed = P(names, None)
    return jax.shard_map(
        per_device,
        mesh=fine,
        in_specs=(placed, placed, placed),
        out_specs=(placed, placed),
        check_vma=False,
    )
```

```python
import functools

import jax
import jax.numpy as jnp
from jax import lax
from jax.experimental import pallas as pl
from jax.experimental.pallas import tpu as pltpu
from jax.sharding import Mesh
from jax.sharding import PartitionSpec as P

logit_scale = 0.125
names = ("y", "zl", "core", "x", "zh")
sizes = (4, 8, 2, 4, 2)
z_axes = ("zh", "zl")
lane = 128
f32 = jnp.float32
bf16 = jnp.bfloat16


def exchange(values, axes):
    return lax.all_to_all(values, axes, 0, 0, tiled=True)


def from_next(values, axis, step):
    n = lax.axis_size(axis)
    return lax.ppermute(values, axis, [(i, (i - step) % n) for i in range(n)])


def bf16_parts(values):
    high = values.astype(bf16)
    return high, (values - high.astype(f32)).astype(bf16)


def along_lanes(column):
    n = column.shape[0]
    at_row = lax.broadcasted_iota(jnp.int32, (n, n), 0)
    at_lane = lax.broadcasted_iota(jnp.int32, (n, n), 1)
    return jnp.sum(jnp.where(at_row == at_lane, column, 0.0), axis=0, keepdims=True)


def first_kernel(sizes, queries_in, teacher_in, sent, queries, teacher, sems):
    ny, nzl, group, nzh, pool = sizes
    copies = [
        pltpu.make_async_copy(teacher_in, teacher, sems.at[0]),
        pltpu.make_async_copy(queries_in, queries, sems.at[1]),
    ]
    for copy in copies:
        copy.start()
    for copy in copies:
        copy.wait()
    for zh in range(nzh):
        for zl in range(nzl):
            to = zh * nzl + zl
            for y in range(ny):
                for i in range(group):
                    at = (((y * nzl + zl) * group + i) * nzh + zh) * pool
                    into = (y * group + i) * pool
                    sent[to, :, into : into + pool] = teacher[:, at : at + pool]
            sent[to, :, ny * group * pool :] = queries[...]


def layout_kernel(nc, nx, place, got, block, high, low, stats, *rows):
    count, dim = block.shape
    group = nc * nx
    block[...] = got[:, group * lane :]
    taught = []
    for i in range(group):
        c, k = divmod(i, nx)
        at = (place[0] + c) % nc * nx + (place[1] + k) % nx
        column = got[:, pl.ds(pl.multiple_of(at * lane, lane), lane)]
        rows[-k % nx][:, dim + c * lane : dim + (c + 1) * lane] = column
        taught.append(column.astype(f32))
    for row in rows:
        row[:, :dim] = block[...]
    taught = jnp.concatenate(taught, axis=1)
    top = jnp.max(taught, axis=1, keepdims=True)
    lifted = jnp.exp(taught - top)
    high[...], low[...] = bf16_parts(lifted)
    stats[...] = jnp.concatenate(
        [along_lanes(top), along_lanes(jnp.sum(lifted, axis=1, keepdims=True))]
        + [jnp.zeros((stats.shape[0] - 2, count), f32)],
        axis=0,
    )


def parts_kernel(block, high, low, taught, near, far, sent):
    ny, width, _ = sent.shape
    count, dim = block.shape
    half = near.shape[0]
    rows = block[...]
    shared = near[...], far[...]
    student = [
        logit_scale * lax.dot_general(rows, p, (((1,), (1,)), ((), ())), preferred_element_type=f32)
        for p in shared
    ]
    top = jnp.maximum(*[jnp.max(v, axis=1, keepdims=True) for v in student])
    total = jnp.zeros_like(top)
    stacked = jnp.zeros((4 * count, dim), f32)
    for i, p in enumerate(shared):
        lifted = jnp.exp(student[i] - top)
        total += jnp.sum(lifted, axis=1, keepdims=True)
        pieces = bf16_parts(lifted) + tuple(v[:, i * half : (i + 1) * half] for v in (high, low))
        stacked += jnp.dot(jnp.concatenate(pieces, axis=0), p, preferred_element_type=f32)
    parts = [
        stacked[at * count : (at + 1) * count] + stacked[(at + 1) * count : (at + 2) * count] for at in (0, 2)
    ]
    mine = [along_lanes(top), along_lanes(total)]
    spread = jnp.concatenate(mine + [taught[: width - 2]], axis=0)
    for y in range(ny):
        for at in range(2):
            sent[y, :, at * dim : (at + 1) * dim] = parts[at][y * width : (y + 1) * width]
        sent[y, :, 2 * dim :] = spread


def merged(pairs):
    high = functools.reduce(jnp.maximum, [top for top, _ in pairs])
    weights = [jnp.exp(top - high) for top, _ in pairs]
    total = functools.reduce(jnp.add, [w * t for w, (_, t) in zip(weights, pairs)])
    return weights, high, total


def stats_place(own, count, i):
    rows = min(own, 4)
    row, at = divmod(i, 4 // rows)
    return row, at * count


def middle_kernel(place, got, sent):
    nz, own, _ = sent.shape
    ny, width, full = got.shape
    count = ny * width
    dim = (full - count) // 2
    at_lane = lax.broadcasted_iota(jnp.int32, (width, count), 1)
    at_row = lax.broadcasted_iota(jnp.int32, (width, count), 0)
    mine = at_lane == at_row + place[0] * width
    stats = []
    for at in range(2):
        pairs = [
            tuple(got[y, 2 * at + i : 2 * at + i + 1, 2 * dim :] for i in range(2)) for y in range(ny)
        ]
        weights, high, total = merged(pairs)
        stats += [high, total]
        part = jnp.zeros((width, dim), f32)
        for y, weight in enumerate(weights):
            column = jnp.sum(jnp.where(mine, weight, 0.0), axis=1, keepdims=True)
            part += column * got[y, :, at * dim : (at + 1) * dim]
        for z in range(nz):
            sent[z, :, at * dim : (at + 1) * dim] = part[z * own : (z + 1) * own]
    for i, values in enumerate(stats):
        row, at = stats_place(own, count, i)
        for z in range(nz):
            sent[z, row : row + 1, 2 * dim + at : 2 * dim + at + count] = values


def all_pairs(got, dim, count, kind):
    nz, own, _ = got.shape
    pairs = []
    for z in range(nz):
        pair = []
        for i in (2 * kind, 2 * kind + 1):
            row, at = stats_place(own, count, i)
            pair.append(got[z, row : row + 1, 2 * dim + at : 2 * dim + at + count])
        pairs.append(pair)
    return pairs


def after_kernel(dim, got, sent):
    group, _, count = sent.shape
    stats = [v for kind in range(2) for v in merged(all_pairs(got, dim, count, kind))[1:]]
    stats = jnp.concatenate(stats, axis=0)
    for i in range(group):
        sent[i] = stats


def query_kernel(count, place, got, grads):
    own, dim = grads.shape
    at_lane = lax.broadcasted_iota(jnp.int32, (own, count), 1)
    at_row = lax.broadcasted_iota(jnp.int32, (own, count), 0)
    mine = at_lane == at_row + place[0]

    def column(values):
        return jnp.sum(jnp.where(mine, values, 0.0), axis=1, keepdims=True)

    parts = []
    for kind in range(2):
        weights, _, total = merged(all_pairs(got, dim, count, kind))
        part = jnp.zeros((own, dim), f32)
        for z, weight in enumerate(weights):
            part += column(weight) * got[z, :, kind * dim : (kind + 1) * dim]
        parts.append(part / column(total))
    grads[...] = logit_scale * (parts[0] - parts[1])


def own_kernel(passages, rows, lifted, tops):
    pool, dim = passages.shape
    own = passages[...]
    for at in range(0, rows.shape[0], 2 * lane):
        at = slice(at, at + 2 * lane)
        student = logit_scale * lax.dot_general(
            own, rows[at, :dim], (((1,), (1,)), ((), ())), preferred_element_type=f32
        )
        taught = rows[at, dim : dim + pool].astype(f32).T
        for which, values in enumerate((student, taught)):
            top = jnp.max(values, axis=0, keepdims=True)
            lifted[which, :, at] = jnp.exp(values - top)
            tops[which : which + 1, at] = top


def last_kernel(nc, nx, place, got, lifted, tops, rows, grads):
    count = got.shape[2]
    pool, dim = grads.shape
    total = jnp.zeros((2 * pool, dim), f32)
    for i in range(0, nc * nx, 2):
        pieces = []
        for j in (i, i + 1):
            c, k = divmod(j, nx)
            at = slice(j * count, (j + 1) * count)
            stats = got[(place[1] + k) % nx * nc + (place[0] + c) % nc]
            weight_s = logit_scale * jnp.exp(tops[0:1, at] - stats[0:1]) / stats[1:2]
            weight_t = logit_scale * jnp.exp(tops[1:2, at] - stats[2:3]) / stats[3:4]
            grad = weight_s * lifted[0, :, at] - weight_t * lifted[1, :, at]
            pieces.append(jnp.concatenate(bf16_parts(grad), axis=0))
        total += jnp.dot(
            jnp.concatenate(pieces, axis=1),
            rows[i * count : (i + 2) * count, :dim],
            preferred_element_type=f32,
        )
    grads[...] = total[:pool] + total[pool:]


vmem = pl.BlockSpec(memory_space=pltpu.VMEM)


def first_buffer(queries, teacher, sizes):
    ny, nzl, group, nzh, pool = sizes
    own, dim = queries.shape
    return pl.pallas_call(
        functools.partial(first_kernel, sizes),
        out_shape=jax.ShapeDtypeStruct((nzh * nzl, own, ny * group * pool + dim), bf16),
        in_specs=[pl.BlockSpec(memory_space=pltpu.HBM)] * 2,
        out_specs=vmem,
        scratch_shapes=[
            pltpu.VMEM(queries.shape, bf16),
            pltpu.VMEM(teacher.shape, bf16),
            pltpu.SemaphoreType.DMA((2,)),
        ],
        compiler_params=pltpu.CompilerParams(vmem_limit_bytes=60 * 2**20),
        cost_estimate=pl.CostEstimate(flops=0, bytes_accessed=2**20, transcendentals=0),
    )(queries, teacher)


def place_of():
    return jnp.stack([lax.axis_index("core"), lax.axis_index("x")]).astype(jnp.int32)


def laid_out(got, sizes):
    ny, width, nc, nx, pool, dim = sizes
    count, group = ny * width, nc * nx
    place = place_of()
    lifted = jax.ShapeDtypeStruct((count, group * pool), bf16)
    row = jax.ShapeDtypeStruct((count, dim + nc * pool), bf16)
    block = jax.ShapeDtypeStruct((count, dim), bf16)
    stats = jax.ShapeDtypeStruct((width, count), f32)
    return pl.pallas_call(
        functools.partial(layout_kernel, nc, nx),
        out_shape=(block, lifted, lifted, stats) + (row,) * nx,
        in_specs=[pl.BlockSpec(memory_space=pltpu.SMEM), vmem],
        out_specs=(vmem,) * (4 + nx),
        compiler_params=pltpu.CompilerParams(vmem_limit_bytes=16 * 2**20),
        cost_estimate=pl.CostEstimate(
            flops=30 * 10**9, bytes_accessed=32 * 2**20, transcendentals=0
        ),
    )(place, got)


def local_parts(block, high, low, stats, near, far, ny):
    count, dim = block.shape
    return pl.pallas_call(
        parts_kernel,
        out_shape=jax.ShapeDtypeStruct((ny, count // ny, 2 * dim + count), f32),
        in_specs=[vmem] * 6,
        out_specs=vmem,
        compiler_params=pltpu.CompilerParams(vmem_limit_bytes=16 * 2**20),
        cost_estimate=pl.CostEstimate(
            flops=10 * count * high.shape[1] * dim,
            bytes_accessed=4 * 2**20,
            transcendentals=count * high.shape[1],
        ),
    )(block, high, low, stats, near.reshape(-1, dim), far.reshape(-1, dim))


def simple_call(kernel, out, scalars, arrays, flops=0):
    smem = pl.BlockSpec(memory_space=pltpu.SMEM)
    return pl.pallas_call(
        kernel,
        out_shape=out,
        in_specs=[smem] * len(scalars) + [vmem] * len(arrays),
        out_specs=(vmem,) * len(out) if isinstance(out, tuple) else vmem,
        compiler_params=pltpu.CompilerParams(vmem_limit_bytes=16 * 2**20),
        cost_estimate=pl.CostEstimate(flops=flops, bytes_accessed=2**16, transcendentals=0),
    )(*scalars, *arrays)


def per_device(queries, passages, teacher):
    own, dim = queries.shape
    pool = passages.shape[0]
    ny, nzl, nc, nx, nzh = (lax.axis_size(a) for a in names)
    nz, group = nzh * nzl, nc * nx

    near = [from_next(passages, "x", k) for k in range(1, nx)]

    got = exchange(first_buffer(queries, teacher, (ny, nzl, group, nzh, pool)), z_axes)
    got, *near = lax.optimization_barrier((got, *near))
    width, count = nz * own, ny * nz * own
    got = got.reshape(width, -1)
    tiles = [got[:, i * group * pool : (i + 1) * group * pool] for i in range(ny)]
    sent = jnp.stack([jnp.concatenate([t, got[:, ny * group * pool :]], axis=1) for t in tiles])
    got = exchange(sent, "y")
    *near, _ = lax.optimization_barrier((*near, sent))
    near = jnp.stack([passages, *near])
    far = from_next(near, "core", 1)
    block, high, low, stats, *rows = laid_out(got.reshape(count, -1), (ny, width, nc, nx, pool, dim))
    parts = local_parts(block, high, low, stats, near, far, ny)

    for k in range(1, nx - 1):
        rows[k] = from_next(rows[k], "x", k)

    z_at = lax.axis_index("y") * width + lax.axis_index(z_axes) * own
    extra = 4 // min(own, 4) * count
    sent = simple_call(
        middle_kernel,
        jax.ShapeDtypeStruct((nz, own, 2 * dim + extra), f32),
        [lax.axis_index("y").astype(jnp.int32)[None]],
        [exchange(parts, "y")],
    )
    got = exchange(sent, z_axes)
    *rows, _ = lax.optimization_barrier((*rows, sent))
    rows[-1] = from_next(rows[-1], "x", nx - 1)

    kept = jnp.stack([r[:, : dim + pool] for r in rows])
    away = jnp.stack([jnp.concatenate([r[:, :dim], r[:, dim + pool :]], axis=1) for r in rows])
    every_row = jnp.concatenate([kept, from_next(away, "core", 1)]).reshape(group * count, dim + pool)

    lifted = jax.ShapeDtypeStruct((2, pool, group * count), f32)
    tops = jax.ShapeDtypeStruct((2, group * count), f32)
    sets = simple_call(own_kernel, (lifted, tops), [], [passages, every_row], flops=2 * pool * group * count * dim)
    every = simple_call(
        functools.partial(after_kernel, dim), jax.ShapeDtypeStruct((group, 4, count), f32), [], [got]
    )
    got, _ = lax.optimization_barrier((got, every))
    every = exchange(every, ("x", "core"))
    query_grad = simple_call(
        functools.partial(query_kernel, count),
        jax.ShapeDtypeStruct((own, dim), f32),
        [z_at.astype(jnp.int32)[None]],
        [got],
    )

    passage_grad = simple_call(
        functools.partial(last_kernel, nc, nx),
        jax.ShapeDtypeStruct((pool, dim), f32),
        [place_of()],
        [every, *sets, every_row],
    )
    return query_grad, passage_grad


def solution(mesh):
    shape = sizes if mesh.devices.size == 512 else (2,) * 5
    fine = Mesh(mesh.devices.reshape(shape), names)
    placed = P(names, None)
    return jax.shard_map(
        per_device,
        mesh=fine,
        in_specs=(placed, placed, placed),
        out_specs=(placed, placed),
        check_vma=False,
    )
```

```python
import functools

import jax
import jax.numpy as jnp
from jax import lax
from jax.experimental import pallas as pl
from jax.experimental.pallas import tpu as pltpu
from jax.sharding import Mesh
from jax.sharding import PartitionSpec as P

logit_scale = 0.125
names = ("y", "zl", "core", "x", "zh")
sizes = (4, 8, 2, 4, 2)
z_axes = ("zh", "zl")
lane = 128
f32 = jnp.float32
bf16 = jnp.bfloat16


def exchange(values, axes):
    return lax.all_to_all(values, axes, 0, 0, tiled=True)


def from_next(values, axis, step):
    n = lax.axis_size(axis)
    return lax.ppermute(values, axis, [(i, (i - step) % n) for i in range(n)])


def bf16_parts(values):
    high = values.astype(bf16)
    return high, (values - high.astype(f32)).astype(bf16)


def along_lanes(column):
    n = column.shape[0]
    at_row = lax.broadcasted_iota(jnp.int32, (n, n), 0)
    at_lane = lax.broadcasted_iota(jnp.int32, (n, n), 1)
    return jnp.sum(jnp.where(at_row == at_lane, column, 0.0), axis=0, keepdims=True)


def first_kernel(sizes, queries_in, teacher_in, sent, queries, teacher, sems):
    ny, nzl, group, nzh, pool = sizes
    copies = [
        pltpu.make_async_copy(teacher_in, teacher, sems.at[0]),
        pltpu.make_async_copy(queries_in, queries, sems.at[1]),
    ]
    for copy in copies:
        copy.start()
    for copy in copies:
        copy.wait()
    for zh in range(nzh):
        for zl in range(nzl):
            to = zh * nzl + zl
            for y in range(ny):
                for i in range(group):
                    at = (((y * nzl + zl) * group + i) * nzh + zh) * pool
                    into = (y * group + i) * pool
                    sent[to, :, into : into + pool] = teacher[:, at : at + pool]
            sent[to, :, ny * group * pool :] = queries[...]


def layout_kernel(nc, nx, place, got, block, high, low, stats, *rows):
    count, dim = block.shape
    group = nc * nx
    block[...] = got[:, group * lane :]
    taught = []
    for i in range(group):
        c, k = divmod(i, nx)
        at = (place[0] + c) % nc * nx + (place[1] + k) % nx
        column = got[:, pl.ds(pl.multiple_of(at * lane, lane), lane)]
        to = rows[-k % nx]
        at = to.shape[1] - (nc - c) * lane
        to[:, at : at + lane] = column
        taught.append(column.astype(f32))
    for row in rows[1:]:
        row[:, :dim] = block[...]
    taught = jnp.concatenate(taught, axis=1)
    top = jnp.max(taught, axis=1, keepdims=True)
    lifted = jnp.exp(taught - top)
    high[...], low[...] = bf16_parts(lifted)
    stats[...] = jnp.concatenate(
        [along_lanes(top), along_lanes(jnp.sum(lifted, axis=1, keepdims=True))]
        + [jnp.zeros((stats.shape[0] - 2, count), f32)],
        axis=0,
    )


def parts_kernel(block, high, low, taught, near, far, sent):
    ny, width, _ = sent.shape
    count, dim = block.shape
    half = near.shape[0]
    rows = block[...]
    shared = near[...], far[...]
    student = [
        logit_scale * lax.dot_general(rows, p, (((1,), (1,)), ((), ())), preferred_element_type=f32)
        for p in shared
    ]
    top = jnp.maximum(*[jnp.max(v, axis=1, keepdims=True) for v in student])
    total = jnp.zeros_like(top)
    products = []
    for i, p in enumerate(shared):
        lifted = jnp.exp(student[i] - top)
        total += jnp.sum(lifted, axis=1, keepdims=True)
        pieces = bf16_parts(lifted) + tuple(v[:, i * half : (i + 1) * half] for v in (high, low))
        products.append(jnp.dot(jnp.concatenate(pieces, axis=0), p, preferred_element_type=f32))
    stacked = products[0] + products[1]
    parts = [
        stacked[at * count : (at + 1) * count] + stacked[(at + 1) * count : (at + 2) * count] for at in (0, 2)
    ]
    mine = [along_lanes(top), along_lanes(total)]
    spread = jnp.concatenate(mine + [taught[: width - 2]], axis=0)
    for y in range(ny):
        for at in range(2):
            sent[y, :, at * dim : (at + 1) * dim] = parts[at][y * width : (y + 1) * width]
        sent[y, :, 2 * dim :] = spread


def merged(pairs):
    high = functools.reduce(jnp.maximum, [top for top, _ in pairs])
    weights = [jnp.exp(top - high) for top, _ in pairs]
    total = functools.reduce(jnp.add, [w * t for w, (_, t) in zip(weights, pairs)])
    return weights, high, total


def stats_place(own, count, i):
    rows = min(own, 4)
    row, at = divmod(i, 4 // rows)
    return row, at * count


def middle_kernel(place, got, sent):
    nz, own, _ = sent.shape
    ny, width, full = got.shape
    count = ny * width
    dim = (full - count) // 2
    at_lane = lax.broadcasted_iota(jnp.int32, (width, count), 1)
    at_row = lax.broadcasted_iota(jnp.int32, (width, count), 0)
    mine = at_lane == at_row + place[0] * width
    stats = []
    for at in range(2):
        pairs = [
            tuple(got[y, 2 * at + i : 2 * at + i + 1, 2 * dim :] for i in range(2)) for y in range(ny)
        ]
        weights, high, total = merged(pairs)
        stats += [high, total]
        part = jnp.zeros((width, dim), f32)
        for y, weight in enumerate(weights):
            column = jnp.sum(jnp.where(mine, weight, 0.0), axis=1, keepdims=True)
            part += column * got[y, :, at * dim : (at + 1) * dim]
        for z in range(nz):
            sent[z, :, at * dim : (at + 1) * dim] = part[z * own : (z + 1) * own]
    for i, values in enumerate(stats):
        row, at = stats_place(own, count, i)
        for z in range(nz):
            sent[z, row : row + 1, 2 * dim + at : 2 * dim + at + count] = values


def all_pairs(got, dim, count, kind):
    nz, own, _ = got.shape
    pairs = []
    for z in range(nz):
        pair = []
        for i in (2 * kind, 2 * kind + 1):
            row, at = stats_place(own, count, i)
            pair.append(got[z, row : row + 1, 2 * dim + at : 2 * dim + at + count])
        pairs.append(pair)
    return pairs


def after_kernel(dim, got, sent):
    group, _, count = sent.shape
    stats = [v for kind in range(2) for v in merged(all_pairs(got, dim, count, kind))[1:]]
    stats = jnp.concatenate(stats, axis=0)
    for i in range(group):
        sent[i] = stats


def query_kernel(count, place, got, grads):
    own, dim = grads.shape
    at_lane = lax.broadcasted_iota(jnp.int32, (own, count), 1)
    at_row = lax.broadcasted_iota(jnp.int32, (own, count), 0)
    mine = at_lane == at_row + place[0]

    def column(values):
        return jnp.sum(jnp.where(mine, values, 0.0), axis=1, keepdims=True)

    parts = []
    for kind in range(2):
        weights, _, total = merged(all_pairs(got, dim, count, kind))
        part = jnp.zeros((own, dim), f32)
        for z, weight in enumerate(weights):
            part += column(weight) * got[z, :, kind * dim : (kind + 1) * dim]
        parts.append(part / column(total))
    grads[...] = logit_scale * (parts[0] - parts[1])


def own_kernel(passages, rows, lifted, tops):
    pool, dim = passages.shape
    own = passages[...]
    for at in range(0, rows.shape[0], 2 * lane):
        at = slice(at, at + 2 * lane)
        student = logit_scale * lax.dot_general(
            own, rows[at, :dim], (((1,), (1,)), ((), ())), preferred_element_type=f32
        )
        taught = rows[at, dim : dim + pool].astype(f32).T
        for which, values in enumerate((student, taught)):
            top = jnp.max(values, axis=0, keepdims=True)
            lifted[which, :, at] = jnp.exp(values - top)
            tops[which : which + 1, at] = top


def last_kernel(nc, nx, place, got, lifted, tops, rows, grads):
    count = got.shape[2]
    pool, dim = grads.shape
    pieces = []
    for i in range(nc * nx):
        c, k = divmod(i, nx)
        at = slice(i * count, (i + 1) * count)
        stats = got[(place[1] + k) % nx * nc + (place[0] + c) % nc]
        weight_s = logit_scale * jnp.exp(tops[0:1, at] - stats[0:1]) / stats[1:2]
        weight_t = logit_scale * jnp.exp(tops[1:2, at] - stats[2:3]) / stats[3:4]
        grad = weight_s * lifted[0, :, at] - weight_t * lifted[1, :, at]
        pieces.append(jnp.concatenate(bf16_parts(grad), axis=0))
    total = jnp.dot(
        jnp.concatenate(pieces, axis=1), rows[:, :dim], preferred_element_type=f32
    )
    grads[...] = total[:pool] + total[pool:]


vmem = pl.BlockSpec(memory_space=pltpu.VMEM)


def first_buffer(queries, teacher, sizes):
    ny, nzl, group, nzh, pool = sizes
    own, dim = queries.shape
    return pl.pallas_call(
        functools.partial(first_kernel, sizes),
        out_shape=jax.ShapeDtypeStruct((nzh * nzl, own, ny * group * pool + dim), bf16),
        in_specs=[pl.BlockSpec(memory_space=pltpu.HBM)] * 2,
        out_specs=vmem,
        scratch_shapes=[
            pltpu.VMEM(queries.shape, bf16),
            pltpu.VMEM(teacher.shape, bf16),
            pltpu.SemaphoreType.DMA((2,)),
        ],
        compiler_params=pltpu.CompilerParams(vmem_limit_bytes=60 * 2**20),
        cost_estimate=pl.CostEstimate(flops=0, bytes_accessed=2**20, transcendentals=0),
    )(queries, teacher)


def place_of():
    return jnp.stack([lax.axis_index("core"), lax.axis_index("x")]).astype(jnp.int32)


def laid_out(got, sizes):
    ny, width, nc, nx, pool, dim = sizes
    count, group = ny * width, nc * nx
    place = place_of()
    lifted = jax.ShapeDtypeStruct((count, group * pool), bf16)
    row = jax.ShapeDtypeStruct((count, dim + nc * pool), bf16)
    mine = jax.ShapeDtypeStruct((count, nc * pool), bf16)
    block = jax.ShapeDtypeStruct((count, dim), bf16)
    stats = jax.ShapeDtypeStruct((width, count), f32)
    return pl.pallas_call(
        functools.partial(layout_kernel, nc, nx),
        out_shape=(block, lifted, lifted, stats, mine) + (row,) * (nx - 1),
        in_specs=[pl.BlockSpec(memory_space=pltpu.SMEM), vmem],
        out_specs=(vmem,) * (4 + nx),
        compiler_params=pltpu.CompilerParams(vmem_limit_bytes=16 * 2**20),
        cost_estimate=pl.CostEstimate(
            flops=30 * 10**9, bytes_accessed=32 * 2**20, transcendentals=0
        ),
    )(place, got)


def local_parts(block, high, low, stats, near, far, ny):
    count, dim = block.shape
    return pl.pallas_call(
        parts_kernel,
        out_shape=jax.ShapeDtypeStruct((ny, count // ny, 2 * dim + count), f32),
        in_specs=[vmem] * 6,
        out_specs=vmem,
        compiler_params=pltpu.CompilerParams(vmem_limit_bytes=16 * 2**20),
        cost_estimate=pl.CostEstimate(
            flops=10 * count * high.shape[1] * dim,
            bytes_accessed=4 * 2**20,
            transcendentals=count * high.shape[1],
        ),
    )(block, high, low, stats, near.reshape(-1, dim), far.reshape(-1, dim))


def simple_call(kernel, out, scalars, arrays, flops=0):
    smem = pl.BlockSpec(memory_space=pltpu.SMEM)
    return pl.pallas_call(
        kernel,
        out_shape=out,
        in_specs=[smem] * len(scalars) + [vmem] * len(arrays),
        out_specs=(vmem,) * len(out) if isinstance(out, tuple) else vmem,
        compiler_params=pltpu.CompilerParams(vmem_limit_bytes=16 * 2**20),
        cost_estimate=pl.CostEstimate(flops=flops, bytes_accessed=2**16, transcendentals=0),
    )(*scalars, *arrays)


def per_device(queries, passages, teacher):
    own, dim = queries.shape
    pool = passages.shape[0]
    ny, nzl, nc, nx, nzh = (lax.axis_size(a) for a in names)
    nz, group = nzh * nzl, nc * nx

    near = [from_next(passages, "x", k) for k in range(1, nx)]

    got = exchange(first_buffer(queries, teacher, (ny, nzl, group, nzh, pool)), z_axes)
    got, *near = lax.optimization_barrier((got, *near))
    width, count = nz * own, ny * nz * own
    got = got.reshape(width, -1)
    tiles = [got[:, i * group * pool : (i + 1) * group * pool] for i in range(ny)]
    sent = jnp.stack([jnp.concatenate([t, got[:, ny * group * pool :]], axis=1) for t in tiles])
    got = exchange(sent, "y")
    *near, _ = lax.optimization_barrier((*near, sent))
    near = jnp.stack([passages, *near])
    far = from_next(near, "core", 1)
    block, high, low, stats, *rows = laid_out(got.reshape(count, -1), (ny, width, nc, nx, pool, dim))
    parts = local_parts(block, high, low, stats, near, far, ny)

    for k in range(1, nx - 1):
        rows[k] = from_next(rows[k], "x", k)

    z_at = lax.axis_index("y") * width + lax.axis_index(z_axes) * own
    extra = 4 // min(own, 4) * count
    sent = simple_call(
        middle_kernel,
        jax.ShapeDtypeStruct((nz, own, 2 * dim + extra), f32),
        [lax.axis_index("y").astype(jnp.int32)[None]],
        [exchange(parts, "y")],
    )
    got = exchange(sent, z_axes)
    rows[0] = jnp.concatenate([block, rows[0]], axis=1)
    *rows, _ = lax.optimization_barrier((*rows, sent))
    rows[-1] = from_next(rows[-1], "x", nx - 1)

    kept = jnp.stack([r[:, : dim + pool] for r in rows])
    away = jnp.stack([jnp.concatenate([r[:, :dim], r[:, dim + pool :]], axis=1) for r in rows])
    every_row = jnp.concatenate([kept, from_next(away, "core", 1)]).reshape(group * count, dim + pool)

    lifted = jax.ShapeDtypeStruct((2, pool, group * count), f32)
    tops = jax.ShapeDtypeStruct((2, group * count), f32)
    sets = simple_call(own_kernel, (lifted, tops), [], [passages, every_row], flops=2 * pool * group * count * dim)
    every = simple_call(
        functools.partial(after_kernel, dim), jax.ShapeDtypeStruct((group, 4, count), f32), [], [got]
    )
    got, _ = lax.optimization_barrier((got, every))
    every = exchange(every, ("x", "core"))
    query_grad = simple_call(
        functools.partial(query_kernel, count),
        jax.ShapeDtypeStruct((own, dim), f32),
        [z_at.astype(jnp.int32)[None]],
        [got],
    )

    passage_grad = simple_call(
        functools.partial(last_kernel, nc, nx),
        jax.ShapeDtypeStruct((pool, dim), f32),
        [place_of()],
        [every, *sets, every_row],
    )
    return query_grad, passage_grad


def solution(mesh):
    shape = sizes if mesh.devices.size == 512 else (2,) * 5
    fine = Mesh(mesh.devices.reshape(shape), names)
    placed = P(names, None)
    return jax.shard_map(
        per_device,
        mesh=fine,
        in_specs=(placed, placed, placed),
        out_specs=(placed, placed),
        check_vma=False,
    )
```

```python
import functools

import jax
import jax.numpy as jnp
from jax import lax
from jax.experimental import pallas as pl
from jax.experimental.pallas import tpu as pltpu
from jax.sharding import Mesh
from jax.sharding import PartitionSpec as P

logit_scale = 0.125
names = ("y", "zl", "core", "x", "zh")
sizes = (4, 8, 2, 4, 2)
z_axes = ("zh", "zl")
lane = 128
f32 = jnp.float32
bf16 = jnp.bfloat16


def exchange(values, axes):
    return lax.all_to_all(values, axes, 0, 0, tiled=True)


def from_next(values, axis, step):
    n = lax.axis_size(axis)
    return lax.ppermute(values, axis, [(i, (i - step) % n) for i in range(n)])


def bf16_parts(values):
    high = values.astype(bf16)
    return high, (values - high.astype(f32)).astype(bf16)


def along_lanes(column):
    n = column.shape[0]
    at_row = lax.broadcasted_iota(jnp.int32, (n, n), 0)
    at_lane = lax.broadcasted_iota(jnp.int32, (n, n), 1)
    return jnp.sum(jnp.where(at_row == at_lane, column, 0.0), axis=0, keepdims=True)


def first_kernel(sizes, queries_in, teacher_in, sent, queries, teacher, sems):
    ny, nzl, group, nzh, pool = sizes
    copies = [
        pltpu.make_async_copy(teacher_in, teacher, sems.at[0]),
        pltpu.make_async_copy(queries_in, queries, sems.at[1]),
    ]
    for copy in copies:
        copy.start()
    for copy in copies:
        copy.wait()
    for zh in range(nzh):
        for zl in range(nzl):
            to = zh * nzl + zl
            for y in range(ny):
                for i in range(group):
                    at = (((y * nzl + zl) * group + i) * nzh + zh) * pool
                    into = (y * group + i) * pool
                    sent[to, :, into : into + pool] = teacher[:, at : at + pool]
            sent[to, :, ny * group * pool :] = queries[...]


def layout_kernel(nc, nx, place, got, block, high, low, stats, *rows):
    count, dim = block.shape
    group = nc * nx
    block[...] = got[:, group * lane :]
    taught = []
    for i in range(group):
        c, k = divmod(i, nx)
        at = (place[0] + c) % nc * nx + (place[1] + k) % nx
        column = got[:, pl.ds(pl.multiple_of(at * lane, lane), lane)]
        to = rows[-k % nx]
        at = to.shape[1] - (nc - c) * lane
        to[:, at : at + lane] = column
        taught.append(column.astype(f32))
    for row in rows[1:]:
        row[:, :dim] = block[...]
    taught = jnp.concatenate(taught, axis=1)
    top = jnp.max(taught, axis=1, keepdims=True)
    lifted = jnp.exp(taught - top)
    high[...], low[...] = bf16_parts(lifted)
    stats[...] = jnp.concatenate(
        [along_lanes(top), along_lanes(jnp.sum(lifted, axis=1, keepdims=True))]
        + [jnp.zeros((stats.shape[0] - 2, count), f32)],
        axis=0,
    )


def parts_kernel(block, high, low, taught, near, far, sent):
    ny, width, _ = sent.shape
    count, dim = block.shape
    half = near.shape[0]
    rows = block[...]
    shared = near[...], far[...]
    student = [
        logit_scale * lax.dot_general(rows, p, (((1,), (1,)), ((), ())), preferred_element_type=f32)
        for p in shared
    ]
    top = jnp.maximum(*[jnp.max(v, axis=1, keepdims=True) for v in student])
    total = jnp.zeros_like(top)
    products = []
    for i, p in enumerate(shared):
        lifted = jnp.exp(student[i] - top)
        total += jnp.sum(lifted, axis=1, keepdims=True)
        pieces = bf16_parts(lifted) + tuple(v[:, i * half : (i + 1) * half] for v in (high, low))
        products.append(jnp.dot(jnp.concatenate(pieces, axis=0), p, preferred_element_type=f32))
    stacked = products[0] + products[1]
    parts = [
        stacked[at * count : (at + 1) * count] + stacked[(at + 1) * count : (at + 2) * count] for at in (0, 2)
    ]
    mine = [along_lanes(top), along_lanes(total)]
    spread = jnp.concatenate(mine + [taught[: width - 2]], axis=0)
    for y in range(ny):
        for at in range(2):
            sent[y, :, at * dim : (at + 1) * dim] = parts[at][y * width : (y + 1) * width]
        sent[y, :, 2 * dim :] = spread


def merged(pairs):
    high = functools.reduce(jnp.maximum, [top for top, _ in pairs])
    weights = [jnp.exp(top - high) for top, _ in pairs]
    total = functools.reduce(jnp.add, [w * t for w, (_, t) in zip(weights, pairs)])
    return weights, high, total


def stats_place(own, count, i):
    rows = min(own, 4)
    row, at = divmod(i, 4 // rows)
    return row, at * count


def middle_kernel(place, got, sent):
    nz, own, _ = sent.shape
    ny, width, full = got.shape
    count = ny * width
    dim = (full - count) // 2
    at_lane = lax.broadcasted_iota(jnp.int32, (width, count), 1)
    at_row = lax.broadcasted_iota(jnp.int32, (width, count), 0)
    mine = at_lane == at_row + place[0] * width
    stats = []
    for at in range(2):
        pairs = [
            tuple(got[y, 2 * at + i : 2 * at + i + 1, 2 * dim :] for i in range(2)) for y in range(ny)
        ]
        weights, high, total = merged(pairs)
        stats += [high, total]
        part = jnp.zeros((width, dim), f32)
        for y, weight in enumerate(weights):
            column = jnp.sum(jnp.where(mine, weight, 0.0), axis=1, keepdims=True)
            part += column * got[y, :, at * dim : (at + 1) * dim]
        for z in range(nz):
            sent[z, :, at * dim : (at + 1) * dim] = part[z * own : (z + 1) * own]
    for i, values in enumerate(stats):
        row, at = stats_place(own, count, i)
        for z in range(nz):
            sent[z, row : row + 1, 2 * dim + at : 2 * dim + at + count] = values


def all_pairs(got, dim, count, kind):
    nz, own, _ = got.shape
    pairs = []
    for z in range(nz):
        pair = []
        for i in (2 * kind, 2 * kind + 1):
            row, at = stats_place(own, count, i)
            pair.append(got[z, row : row + 1, 2 * dim + at : 2 * dim + at + count])
        pairs.append(pair)
    return pairs


def after_kernel(dim, got, sent):
    group, _, count = sent.shape
    stats = [v for kind in range(2) for v in merged(all_pairs(got, dim, count, kind))[1:]]
    stats = jnp.concatenate(stats, axis=0)
    for i in range(group):
        sent[i] = stats


def query_kernel(count, place, got, grads):
    own, dim = grads.shape
    at_lane = lax.broadcasted_iota(jnp.int32, (own, count), 1)
    at_row = lax.broadcasted_iota(jnp.int32, (own, count), 0)
    mine = at_lane == at_row + place[0]

    def column(values):
        return jnp.sum(jnp.where(mine, values, 0.0), axis=1, keepdims=True)

    parts = []
    for kind in range(2):
        weights, _, total = merged(all_pairs(got, dim, count, kind))
        part = jnp.zeros((own, dim), f32)
        for z, weight in enumerate(weights):
            part += column(weight) * got[z, :, kind * dim : (kind + 1) * dim]
        parts.append(part / column(total))
    grads[...] = logit_scale * (parts[0] - parts[1])


def own_kernel(passages, rows, lifted, tops):
    pool, dim = passages.shape
    own = passages[...]
    for at in range(0, rows.shape[0], 2 * lane):
        at = slice(at, at + 2 * lane)
        student = logit_scale * lax.dot_general(
            own, rows[at, :dim], (((1,), (1,)), ((), ())), preferred_element_type=f32
        )
        taught = rows[at, dim : dim + pool].astype(f32).T
        for which, values in enumerate((student, taught)):
            top = jnp.max(values, axis=0, keepdims=True)
            lifted[which, :, at] = jnp.exp(values - top)
            tops[which : which + 1, at] = top


def last_kernel(nc, nx, place, got, lifted, tops, rows, grads):
    count = got.shape[2]
    pool, dim = grads.shape
    pieces = []
    for i in range(nc * nx):
        c, k = divmod(i, nx)
        at = slice(i * count, (i + 1) * count)
        stats = got[(place[1] + k) % nx * nc + (place[0] + c) % nc]
        weight_s = logit_scale * jnp.exp(tops[0:1, at] - stats[0:1]) / stats[1:2]
        weight_t = logit_scale * jnp.exp(tops[1:2, at] - stats[2:3]) / stats[3:4]
        grad = weight_s * lifted[0, :, at] - weight_t * lifted[1, :, at]
        pieces.append(jnp.concatenate(bf16_parts(grad), axis=0))
    total = jnp.dot(
        jnp.concatenate(pieces, axis=1), rows[:, :dim], preferred_element_type=f32
    )
    grads[...] = total[:pool] + total[pool:]


vmem = pl.BlockSpec(memory_space=pltpu.VMEM)


def first_buffer(queries, teacher, sizes):
    ny, nzl, group, nzh, pool = sizes
    own, dim = queries.shape
    return pl.pallas_call(
        functools.partial(first_kernel, sizes),
        out_shape=jax.ShapeDtypeStruct((nzh * nzl, own, ny * group * pool + dim), bf16),
        in_specs=[pl.BlockSpec(memory_space=pltpu.HBM)] * 2,
        out_specs=vmem,
        scratch_shapes=[
            pltpu.VMEM(queries.shape, bf16),
            pltpu.VMEM(teacher.shape, bf16),
            pltpu.SemaphoreType.DMA((2,)),
        ],
        compiler_params=pltpu.CompilerParams(vmem_limit_bytes=60 * 2**20),
        cost_estimate=pl.CostEstimate(flops=0, bytes_accessed=2**20, transcendentals=0),
    )(queries, teacher)


def place_of():
    return jnp.stack([lax.axis_index("core"), lax.axis_index("x")]).astype(jnp.int32)


def laid_out(got, sizes):
    ny, width, nc, nx, pool, dim = sizes
    count, group = ny * width, nc * nx
    place = place_of()
    lifted = jax.ShapeDtypeStruct((count, group * pool), bf16)
    row = jax.ShapeDtypeStruct((count, dim + nc * pool), bf16)
    mine = jax.ShapeDtypeStruct((count, nc * pool), bf16)
    block = jax.ShapeDtypeStruct((count, dim), bf16)
    stats = jax.ShapeDtypeStruct((width, count), f32)
    return pl.pallas_call(
        functools.partial(layout_kernel, nc, nx),
        out_shape=(block, lifted, lifted, stats, mine) + (row,) * (nx - 1),
        in_specs=[pl.BlockSpec(memory_space=pltpu.SMEM), vmem],
        out_specs=(vmem,) * (4 + nx),
        compiler_params=pltpu.CompilerParams(vmem_limit_bytes=16 * 2**20),
        cost_estimate=pl.CostEstimate(
            flops=30 * 10**9, bytes_accessed=32 * 2**20, transcendentals=0
        ),
    )(place, got)


def local_parts(block, high, low, stats, near, far, ny):
    count, dim = block.shape
    return pl.pallas_call(
        parts_kernel,
        out_shape=jax.ShapeDtypeStruct((ny, count // ny, 2 * dim + count), f32),
        in_specs=[vmem] * 6,
        out_specs=vmem,
        compiler_params=pltpu.CompilerParams(vmem_limit_bytes=16 * 2**20),
        cost_estimate=pl.CostEstimate(
            flops=10 * count * high.shape[1] * dim,
            bytes_accessed=4 * 2**20,
            transcendentals=count * high.shape[1],
        ),
    )(block, high, low, stats, near.reshape(-1, dim), far.reshape(-1, dim))


def simple_call(kernel, out, scalars, arrays, flops=0):
    smem = pl.BlockSpec(memory_space=pltpu.SMEM)
    return pl.pallas_call(
        kernel,
        out_shape=out,
        in_specs=[smem] * len(scalars) + [vmem] * len(arrays),
        out_specs=(vmem,) * len(out) if isinstance(out, tuple) else vmem,
        compiler_params=pltpu.CompilerParams(vmem_limit_bytes=16 * 2**20),
        cost_estimate=pl.CostEstimate(flops=flops, bytes_accessed=2**16, transcendentals=0),
    )(*scalars, *arrays)


def per_device(queries, passages, teacher):
    own, dim = queries.shape
    pool = passages.shape[0]
    ny, nzl, nc, nx, nzh = (lax.axis_size(a) for a in names)
    nz, group = nzh * nzl, nc * nx

    near = [from_next(passages, "x", k) for k in range(1, nx)]

    got = exchange(first_buffer(queries, teacher, (ny, nzl, group, nzh, pool)), z_axes)
    got, *near = lax.optimization_barrier((got, *near))
    width, count = nz * own, ny * nz * own
    got = got.reshape(width, -1)
    tiles = [got[:, i * group * pool : (i + 1) * group * pool] for i in range(ny)]
    sent = jnp.stack([jnp.concatenate([t, got[:, ny * group * pool :]], axis=1) for t in tiles])
    got = exchange(sent, "y")
    *near, _ = lax.optimization_barrier((*near, sent))
    near = jnp.stack([passages, *near])
    far = from_next(near, "core", 1)
    block, high, low, stats, *rows = laid_out(got.reshape(count, -1), (ny, width, nc, nx, pool, dim))
    parts = local_parts(block, high, low, stats, near, far, ny)

    for k in range(1, nx - 1):
        rows[k] = from_next(rows[k], "x", k)

    z_at = lax.axis_index("y") * width + lax.axis_index(z_axes) * own
    extra = 4 // min(own, 4) * count
    sent = simple_call(
        middle_kernel,
        jax.ShapeDtypeStruct((nz, own, 2 * dim + extra), f32),
        [lax.axis_index("y").astype(jnp.int32)[None]],
        [exchange(parts, "y")],
    )
    got = exchange(sent, z_axes)
    rows[0] = jnp.concatenate([block, rows[0]], axis=1)
    *rows, _ = lax.optimization_barrier((*rows, sent))
    rows[-1] = from_next(rows[-1], "x", nx - 1)

    kept = jnp.stack([r[:, : dim + pool] for r in rows])
    away = jnp.stack([jnp.concatenate([r[:, :dim], r[:, dim + pool :]], axis=1) for r in rows])
    every_row = jnp.concatenate([kept, from_next(away, "core", 1)]).reshape(group * count, dim + pool)

    lifted = jax.ShapeDtypeStruct((2, pool, group * count), f32)
    tops = jax.ShapeDtypeStruct((2, group * count), f32)
    sets = simple_call(own_kernel, (lifted, tops), [], [passages, every_row], flops=2 * pool * group * count * dim)
    got, *sets = lax.optimization_barrier((got, *sets))
    every = simple_call(
        functools.partial(after_kernel, dim), jax.ShapeDtypeStruct((group, 4, count), f32), [], [got]
    )
    got, _ = lax.optimization_barrier((got, every))
    every = exchange(every, ("x", "core"))
    query_grad = simple_call(
        functools.partial(query_kernel, count),
        jax.ShapeDtypeStruct((own, dim), f32),
        [z_at.astype(jnp.int32)[None]],
        [got],
    )

    passage_grad = simple_call(
        functools.partial(last_kernel, nc, nx),
        jax.ShapeDtypeStruct((pool, dim), f32),
        [place_of()],
        [every, *sets, every_row],
    )
    return query_grad, passage_grad


def solution(mesh):
    shape = sizes if mesh.devices.size == 512 else (2,) * 5
    fine = Mesh(mesh.devices.reshape(shape), names)
    placed = P(names, None)
    return jax.shard_map(
        per_device,
        mesh=fine,
        in_specs=(placed, placed, placed),
        out_specs=(placed, placed),
        check_vma=False,
    )
```

```python
import functools

import jax
import jax.numpy as jnp
from jax import lax
from jax.experimental import pallas as pl
from jax.experimental.pallas import tpu as pltpu
from jax.sharding import Mesh
from jax.sharding import PartitionSpec as P

logit_scale = 0.125
names = ("y", "zl", "core", "x", "zh")
sizes = (4, 8, 2, 4, 2)
z_axes = ("zh", "zl")
lane = 128
f32 = jnp.float32
bf16 = jnp.bfloat16


def exchange(values, axes):
    return lax.all_to_all(values, axes, 0, 0, tiled=True)


def from_next(values, axis, step):
    n = lax.axis_size(axis)
    return lax.ppermute(values, axis, [(i, (i - step) % n) for i in range(n)])


def bf16_parts(values):
    high = values.astype(bf16)
    return high, (values - high.astype(f32)).astype(bf16)


def along_lanes(column):
    n = column.shape[0]
    at_row = lax.broadcasted_iota(jnp.int32, (n, n), 0)
    at_lane = lax.broadcasted_iota(jnp.int32, (n, n), 1)
    return jnp.sum(jnp.where(at_row == at_lane, column, 0.0), axis=0, keepdims=True)


def first_kernel(sizes, queries_in, teacher_in, sent, queries, teacher, sems):
    ny, nzl, group, nzh, pool = sizes
    chunk = nzl * group * nzh * pool
    copies = []
    for y in range(ny):
        at = pl.ds(y * chunk, chunk)
        copies.append(pltpu.make_async_copy(teacher_in.at[:, at], teacher.at[:, at], sems.at[y]))
    copies.append(pltpu.make_async_copy(queries_in, queries, sems.at[ny]))
    for copy in copies:
        copy.start()
    for y in range(ny):
        copies[y].wait()
        for zh in range(nzh):
            for zl in range(nzl):
                for i in range(group):
                    at = (((y * nzl + zl) * group + i) * nzh + zh) * pool
                    into = (y * group + i) * pool
                    sent[zh * nzl + zl, :, into : into + pool] = teacher[:, at : at + pool]
    copies[ny].wait()
    for z in range(nzh * nzl):
        sent[z, :, ny * group * pool :] = queries[...]


def layout_kernel(nc, nx, place, got, block, high, low, stats, *rows):
    count, dim = block.shape
    group = nc * nx
    block[...] = got[:, group * lane :]
    taught = []
    for i in range(group):
        c, k = divmod(i, nx)
        at = (place[0] + c) % nc * nx + (place[1] + k) % nx
        column = got[:, pl.ds(pl.multiple_of(at * lane, lane), lane)]
        to = rows[-k % nx]
        at = to.shape[1] - (nc - c) * lane
        to[:, at : at + lane] = column
        taught.append(column.astype(f32))
    for row in rows[1:]:
        row[:, :dim] = block[...]
    taught = jnp.concatenate(taught, axis=1)
    top = jnp.max(taught, axis=1, keepdims=True)
    lifted = jnp.exp(taught - top)
    high[...], low[...] = bf16_parts(lifted)
    stats[...] = jnp.concatenate(
        [along_lanes(top), along_lanes(jnp.sum(lifted, axis=1, keepdims=True))]
        + [jnp.zeros((stats.shape[0] - 2, count), f32)],
        axis=0,
    )


def parts_kernel(block, high, low, taught, near, far, sent):
    ny, width, _ = sent.shape
    count, dim = block.shape
    half = near.shape[0]
    rows = block[...]
    shared = near[...], far[...]
    student = [
        logit_scale * lax.dot_general(rows, p, (((1,), (1,)), ((), ())), preferred_element_type=f32)
        for p in shared
    ]
    top = jnp.maximum(*[jnp.max(v, axis=1, keepdims=True) for v in student])
    total = jnp.zeros_like(top)
    products = []
    for i, p in enumerate(shared):
        lifted = jnp.exp(student[i] - top)
        total += jnp.sum(lifted, axis=1, keepdims=True)
        pieces = bf16_parts(lifted) + tuple(v[:, i * half : (i + 1) * half] for v in (high, low))
        products.append(jnp.dot(jnp.concatenate(pieces, axis=0), p, preferred_element_type=f32))
    stacked = products[0] + products[1]
    parts = [
        stacked[at * count : (at + 1) * count] + stacked[(at + 1) * count : (at + 2) * count] for at in (0, 2)
    ]
    mine = [along_lanes(top), along_lanes(total)]
    spread = jnp.concatenate(mine + [taught[: width - 2]], axis=0)
    for y in range(ny):
        for at in range(2):
            sent[y, :, at * dim : (at + 1) * dim] = parts[at][y * width : (y + 1) * width]
        sent[y, :, 2 * dim :] = spread


def merged(pairs):
    high = functools.reduce(jnp.maximum, [top for top, _ in pairs])
    weights = [jnp.exp(top - high) for top, _ in pairs]
    total = functools.reduce(jnp.add, [w * t for w, (_, t) in zip(weights, pairs)])
    return weights, high, total


def stats_place(own, count, i):
    rows = min(own, 4)
    row, at = divmod(i, 4 // rows)
    return row, at * count


def middle_kernel(place, got, sent):
    nz, own, _ = sent.shape
    ny, width, full = got.shape
    count = ny * width
    dim = (full - count) // 2
    at_lane = lax.broadcasted_iota(jnp.int32, (width, count), 1)
    at_row = lax.broadcasted_iota(jnp.int32, (width, count), 0)
    mine = at_lane == at_row + place[0] * width
    stats = []
    for at in range(2):
        pairs = [
            tuple(got[y, 2 * at + i : 2 * at + i + 1, 2 * dim :] for i in range(2)) for y in range(ny)
        ]
        weights, high, total = merged(pairs)
        stats += [high, total]
        part = jnp.zeros((width, dim), f32)
        for y, weight in enumerate(weights):
            column = jnp.sum(jnp.where(mine, weight, 0.0), axis=1, keepdims=True)
            part += column * got[y, :, at * dim : (at + 1) * dim]
        for z in range(nz):
            sent[z, :, at * dim : (at + 1) * dim] = part[z * own : (z + 1) * own]
    for i, values in enumerate(stats):
        row, at = stats_place(own, count, i)
        for z in range(nz):
            sent[z, row : row + 1, 2 * dim + at : 2 * dim + at + count] = values


def all_pairs(got, dim, count, kind):
    nz, own, _ = got.shape
    pairs = []
    for z in range(nz):
        pair = []
        for i in (2 * kind, 2 * kind + 1):
            row, at = stats_place(own, count, i)
            pair.append(got[z, row : row + 1, 2 * dim + at : 2 * dim + at + count])
        pairs.append(pair)
    return pairs


def after_kernel(dim, got, sent):
    group, _, count = sent.shape
    stats = [v for kind in range(2) for v in merged(all_pairs(got, dim, count, kind))[1:]]
    stats = jnp.concatenate(stats, axis=0)
    for i in range(group):
        sent[i] = stats


def query_kernel(count, place, got, grads):
    own, dim = grads.shape
    at_lane = lax.broadcasted_iota(jnp.int32, (own, count), 1)
    at_row = lax.broadcasted_iota(jnp.int32, (own, count), 0)
    mine = at_lane == at_row + place[0]

    def column(values):
        return jnp.sum(jnp.where(mine, values, 0.0), axis=1, keepdims=True)

    parts = []
    for kind in range(2):
        weights, _, total = merged(all_pairs(got, dim, count, kind))
        part = jnp.zeros((own, dim), f32)
        for z, weight in enumerate(weights):
            part += column(weight) * got[z, :, kind * dim : (kind + 1) * dim]
        parts.append(part / column(total))
    grads[...] = logit_scale * (parts[0] - parts[1])


def own_kernel(passages, rows, lifted, tops):
    pool, dim = passages.shape
    own = passages[...]
    for at in range(0, rows.shape[0], 2 * lane):
        at = slice(at, at + 2 * lane)
        student = logit_scale * lax.dot_general(
            own, rows[at, :dim], (((1,), (1,)), ((), ())), preferred_element_type=f32
        )
        taught = rows[at, dim : dim + pool].astype(f32).T
        for which, values in enumerate((student, taught)):
            top = jnp.max(values, axis=0, keepdims=True)
            lifted[which, :, at] = jnp.exp(values - top)
            tops[which : which + 1, at] = top


def last_kernel(nc, nx, place, got, lifted, tops, rows, grads):
    count = got.shape[2]
    pool, dim = grads.shape
    pieces = []
    for i in range(nc * nx):
        c, k = divmod(i, nx)
        at = slice(i * count, (i + 1) * count)
        stats = got[(place[1] + k) % nx * nc + (place[0] + c) % nc]
        weight_s = logit_scale * jnp.exp(tops[0:1, at] - stats[0:1]) / stats[1:2]
        weight_t = logit_scale * jnp.exp(tops[1:2, at] - stats[2:3]) / stats[3:4]
        grad = weight_s * lifted[0, :, at] - weight_t * lifted[1, :, at]
        pieces.append(jnp.concatenate(bf16_parts(grad), axis=0))
    total = jnp.dot(
        jnp.concatenate(pieces, axis=1), rows[:, :dim], preferred_element_type=f32
    )
    grads[...] = total[:pool] + total[pool:]


vmem = pl.BlockSpec(memory_space=pltpu.VMEM)


def first_buffer(queries, teacher, sizes):
    ny, nzl, group, nzh, pool = sizes
    own, dim = queries.shape
    return pl.pallas_call(
        functools.partial(first_kernel, sizes),
        out_shape=jax.ShapeDtypeStruct((nzh * nzl, own, ny * group * pool + dim), bf16),
        in_specs=[pl.BlockSpec(memory_space=pltpu.HBM)] * 2,
        out_specs=vmem,
        scratch_shapes=[
            pltpu.VMEM(queries.shape, bf16),
            pltpu.VMEM(teacher.shape, bf16),
            pltpu.SemaphoreType.DMA((ny + 1,)),
        ],
        compiler_params=pltpu.CompilerParams(vmem_limit_bytes=60 * 2**20),
        cost_estimate=pl.CostEstimate(flops=0, bytes_accessed=2**20, transcendentals=0),
    )(queries, teacher)


def place_of():
    return jnp.stack([lax.axis_index("core"), lax.axis_index("x")]).astype(jnp.int32)


def laid_out(got, sizes):
    ny, width, nc, nx, pool, dim = sizes
    count, group = ny * width, nc * nx
    place = place_of()
    lifted = jax.ShapeDtypeStruct((count, group * pool), bf16)
    row = jax.ShapeDtypeStruct((count, dim + nc * pool), bf16)
    mine = jax.ShapeDtypeStruct((count, nc * pool), bf16)
    block = jax.ShapeDtypeStruct((count, dim), bf16)
    stats = jax.ShapeDtypeStruct((width, count), f32)
    return pl.pallas_call(
        functools.partial(layout_kernel, nc, nx),
        out_shape=(block, lifted, lifted, stats, mine) + (row,) * (nx - 1),
        in_specs=[pl.BlockSpec(memory_space=pltpu.SMEM), vmem],
        out_specs=(vmem,) * (4 + nx),
        compiler_params=pltpu.CompilerParams(vmem_limit_bytes=16 * 2**20),
        cost_estimate=pl.CostEstimate(
            flops=30 * 10**9, bytes_accessed=32 * 2**20, transcendentals=0
        ),
    )(place, got)


def local_parts(block, high, low, stats, near, far, ny):
    count, dim = block.shape
    return pl.pallas_call(
        parts_kernel,
        out_shape=jax.ShapeDtypeStruct((ny, count // ny, 2 * dim + count), f32),
        in_specs=[vmem] * 6,
        out_specs=vmem,
        compiler_params=pltpu.CompilerParams(vmem_limit_bytes=16 * 2**20),
        cost_estimate=pl.CostEstimate(
            flops=10 * count * high.shape[1] * dim,
            bytes_accessed=4 * 2**20,
            transcendentals=count * high.shape[1],
        ),
    )(block, high, low, stats, near.reshape(-1, dim), far.reshape(-1, dim))


def simple_call(kernel, out, scalars, arrays, flops=0):
    smem = pl.BlockSpec(memory_space=pltpu.SMEM)
    return pl.pallas_call(
        kernel,
        out_shape=out,
        in_specs=[smem] * len(scalars) + [vmem] * len(arrays),
        out_specs=(vmem,) * len(out) if isinstance(out, tuple) else vmem,
        compiler_params=pltpu.CompilerParams(vmem_limit_bytes=16 * 2**20),
        cost_estimate=pl.CostEstimate(flops=flops, bytes_accessed=2**16, transcendentals=0),
    )(*scalars, *arrays)


def per_device(queries, passages, teacher):
    own, dim = queries.shape
    pool = passages.shape[0]
    ny, nzl, nc, nx, nzh = (lax.axis_size(a) for a in names)
    nz, group = nzh * nzl, nc * nx

    near = [from_next(passages, "x", k) for k in range(1, nx)]

    got = exchange(first_buffer(queries, teacher, (ny, nzl, group, nzh, pool)), z_axes)
    got, *near = lax.optimization_barrier((got, *near))
    width, count = nz * own, ny * nz * own
    got = got.reshape(width, -1)
    tiles = [got[:, i * group * pool : (i + 1) * group * pool] for i in range(ny)]
    sent = jnp.stack([jnp.concatenate([t, got[:, ny * group * pool :]], axis=1) for t in tiles])
    got = exchange(sent, "y")
    *near, _ = lax.optimization_barrier((*near, sent))
    near = jnp.stack([passages, *near])
    far = from_next(near, "core", 1)
    block, high, low, stats, *rows = laid_out(got.reshape(count, -1), (ny, width, nc, nx, pool, dim))
    parts = local_parts(block, high, low, stats, near, far, ny)

    for k in range(1, nx - 1):
        rows[k] = from_next(rows[k], "x", k)

    z_at = lax.axis_index("y") * width + lax.axis_index(z_axes) * own
    extra = 4 // min(own, 4) * count
    sent = simple_call(
        middle_kernel,
        jax.ShapeDtypeStruct((nz, own, 2 * dim + extra), f32),
        [lax.axis_index("y").astype(jnp.int32)[None]],
        [exchange(parts, "y")],
    )
    got = exchange(sent, z_axes)
    rows[0] = jnp.concatenate([block, rows[0]], axis=1)
    *rows, _ = lax.optimization_barrier((*rows, sent))
    rows[-1] = from_next(rows[-1], "x", nx - 1)

    kept = jnp.stack([r[:, : dim + pool] for r in rows])
    away = jnp.stack([jnp.concatenate([r[:, :dim], r[:, dim + pool :]], axis=1) for r in rows])
    every_row = jnp.concatenate([kept, from_next(away, "core", 1)]).reshape(group * count, dim + pool)

    lifted = jax.ShapeDtypeStruct((2, pool, group * count), f32)
    tops = jax.ShapeDtypeStruct((2, group * count), f32)
    sets = simple_call(own_kernel, (lifted, tops), [], [passages, every_row], flops=2 * pool * group * count * dim)
    got, *sets = lax.optimization_barrier((got, *sets))
    every = simple_call(
        functools.partial(after_kernel, dim), jax.ShapeDtypeStruct((group, 4, count), f32), [], [got]
    )
    got, _ = lax.optimization_barrier((got, every))
    every = exchange(every, ("x", "core"))
    query_grad = simple_call(
        functools.partial(query_kernel, count),
        jax.ShapeDtypeStruct((own, dim), f32),
        [z_at.astype(jnp.int32)[None]],
        [got],
    )

    passage_grad = simple_call(
        functools.partial(last_kernel, nc, nx),
        jax.ShapeDtypeStruct((pool, dim), f32),
        [place_of()],
        [every, *sets, every_row],
    )
    return query_grad, passage_grad


def solution(mesh):
    shape = sizes if mesh.devices.size == 512 else (2,) * 5
    fine = Mesh(mesh.devices.reshape(shape), names)
    placed = P(names, None)
    return jax.shard_map(
        per_device,
        mesh=fine,
        in_specs=(placed, placed, placed),
        out_specs=(placed, placed),
        check_vma=False,
    )
```

```python
import functools

import jax
import jax.numpy as jnp
from jax import lax
from jax.experimental import pallas as pl
from jax.experimental.pallas import tpu as pltpu
from jax.sharding import Mesh
from jax.sharding import PartitionSpec as P

logit_scale = 0.125
names = ("y", "zl", "core", "x", "zh")
sizes = (4, 8, 2, 4, 2)
z_axes = ("zh", "zl")
lane = 128
f32 = jnp.float32
bf16 = jnp.bfloat16


def exchange(values, axes):
    return lax.all_to_all(values, axes, 0, 0, tiled=True)


def from_next(values, axis, step):
    n = lax.axis_size(axis)
    return lax.ppermute(values, axis, [(i, (i - step) % n) for i in range(n)])


def bf16_parts(values):
    high = values.astype(bf16)
    return high, (values - high.astype(f32)).astype(bf16)


def along_lanes(column):
    n = column.shape[0]
    at_row = lax.broadcasted_iota(jnp.int32, (n, n), 0)
    at_lane = lax.broadcasted_iota(jnp.int32, (n, n), 1)
    return jnp.sum(jnp.where(at_row == at_lane, column, 0.0), axis=0, keepdims=True)


def first_kernel(sizes, queries_in, teacher_in, sent, queries, teacher, sems):
    ny, nzl, group, nzh, pool = sizes
    copies = [
        pltpu.make_async_copy(teacher_in, teacher, sems.at[0]),
        pltpu.make_async_copy(queries_in, queries, sems.at[1]),
    ]
    for copy in copies:
        copy.start()
    for copy in copies:
        copy.wait()
    for zh in range(nzh):
        for zl in range(nzl):
            to = zh * nzl + zl
            for y in range(ny):
                for i in range(group):
                    at = (((y * nzl + zl) * group + i) * nzh + zh) * pool
                    into = (y * group + i) * pool
                    sent[to, :, into : into + pool] = teacher[:, at : at + pool]
            sent[to, :, ny * group * pool :] = queries[...]


def layout_kernel(nc, nx, place, got, block, high, low, stats, *rows):
    count, dim = block.shape
    group = nc * nx
    block[...] = got[:, group * lane :]
    taught = []
    for i in range(group):
        c, k = divmod(i, nx)
        at = (place[0] + c) % nc * nx + (place[1] + k) % nx
        column = got[:, pl.ds(pl.multiple_of(at * lane, lane), lane)]
        to = rows[-k % nx]
        at = to.shape[1] - (nc - c) * lane
        to[:, at : at + lane] = column
        taught.append(column.astype(f32))
    for row in rows[1:]:
        row[:, :dim] = block[...]
    taught = jnp.concatenate(taught, axis=1)
    top = jnp.max(taught, axis=1, keepdims=True)
    lifted = jnp.exp(taught - top)
    high[...], low[...] = bf16_parts(lifted)
    stats[...] = jnp.concatenate(
        [along_lanes(top), along_lanes(jnp.sum(lifted, axis=1, keepdims=True))]
        + [jnp.zeros((stats.shape[0] - 2, count), f32)],
        axis=0,
    )


def parts_kernel(block, high, low, taught, near, far, sent):
    ny, width, _ = sent.shape
    count, dim = block.shape
    half = near.shape[0]
    rows = block[...]
    shared = near[...], far[...]
    student = [
        logit_scale * lax.dot_general(rows, p, (((1,), (1,)), ((), ())), preferred_element_type=f32)
        for p in shared
    ]
    top = jnp.maximum(*[jnp.max(v, axis=1, keepdims=True) for v in student])
    total = jnp.zeros_like(top)
    products = []
    for i, p in enumerate(shared):
        lifted = jnp.exp(student[i] - top)
        total += jnp.sum(lifted, axis=1, keepdims=True)
        pieces = bf16_parts(lifted) + tuple(v[:, i * half : (i + 1) * half] for v in (high, low))
        products.append(jnp.dot(jnp.concatenate(pieces, axis=0), p, preferred_element_type=f32))
    stacked = products[0] + products[1]
    parts = [
        stacked[at * count : (at + 1) * count] + stacked[(at + 1) * count : (at + 2) * count] for at in (0, 2)
    ]
    mine = [along_lanes(top), along_lanes(total)]
    spread = jnp.concatenate(mine + [taught[: width - 2]], axis=0)
    for y in range(ny):
        for at in range(2):
            sent[y, :, at * dim : (at + 1) * dim] = parts[at][y * width : (y + 1) * width]
        sent[y, :, 2 * dim :] = spread


def merged(pairs):
    high = functools.reduce(jnp.maximum, [top for top, _ in pairs])
    weights = [jnp.exp(top - high) for top, _ in pairs]
    total = functools.reduce(jnp.add, [w * t for w, (_, t) in zip(weights, pairs)])
    return weights, high, total


def stats_place(own, count, i):
    rows = min(own, 4)
    row, at = divmod(i, 4 // rows)
    return row, at * count


def middle_kernel(place, got, sent):
    nz, own, _ = sent.shape
    ny, width, full = got.shape
    count = ny * width
    dim = (full - count) // 2
    at_lane = lax.broadcasted_iota(jnp.int32, (width, count), 1)
    at_row = lax.broadcasted_iota(jnp.int32, (width, count), 0)
    mine = at_lane == at_row + place[0] * width
    stats = []
    for at in range(2):
        pairs = [
            tuple(got[y, 2 * at + i : 2 * at + i + 1, 2 * dim :] for i in range(2)) for y in range(ny)
        ]
        weights, high, total = merged(pairs)
        stats += [high, total]
        part = jnp.zeros((width, dim), f32)
        for y, weight in enumerate(weights):
            column = jnp.sum(jnp.where(mine, weight, 0.0), axis=1, keepdims=True)
            part += column * got[y, :, at * dim : (at + 1) * dim]
        for z in range(nz):
            sent[z, :, at * dim : (at + 1) * dim] = part[z * own : (z + 1) * own]
    for i, values in enumerate(stats):
        row, at = stats_place(own, count, i)
        for z in range(nz):
            sent[z, row : row + 1, 2 * dim + at : 2 * dim + at + count] = values


def all_pairs(got, dim, count, kind):
    nz, own, _ = got.shape
    pairs = []
    for z in range(nz):
        pair = []
        for i in (2 * kind, 2 * kind + 1):
            row, at = stats_place(own, count, i)
            pair.append(got[z, row : row + 1, 2 * dim + at : 2 * dim + at + count])
        pairs.append(pair)
    return pairs


def after_kernel(dim, got, sent):
    group, _, count = sent.shape
    stats = [v for kind in range(2) for v in merged(all_pairs(got, dim, count, kind))[1:]]
    stats = jnp.concatenate(stats, axis=0)
    for i in range(group):
        sent[i] = stats


def query_kernel(count, place, got, grads):
    own, dim = grads.shape
    at_lane = lax.broadcasted_iota(jnp.int32, (own, count), 1)
    at_row = lax.broadcasted_iota(jnp.int32, (own, count), 0)
    mine = at_lane == at_row + place[0]

    def column(values):
        return jnp.sum(jnp.where(mine, values, 0.0), axis=1, keepdims=True)

    parts = []
    for kind in range(2):
        weights, _, total = merged(all_pairs(got, dim, count, kind))
        part = jnp.zeros((own, dim), f32)
        for z, weight in enumerate(weights):
            part += column(weight) * got[z, :, kind * dim : (kind + 1) * dim]
        parts.append(part / column(total))
    grads[...] = logit_scale * (parts[0] - parts[1])


def own_kernel(passages, rows, lifted, tops):
    pool, dim = passages.shape
    own = passages[...]
    for at in range(0, rows.shape[0], 2 * lane):
        at = slice(at, at + 2 * lane)
        student = logit_scale * lax.dot_general(
            own, rows[at, :dim], (((1,), (1,)), ((), ())), preferred_element_type=f32
        )
        taught = rows[at, dim : dim + pool].astype(f32).T
        for which, values in enumerate((student, taught)):
            top = jnp.max(values, axis=0, keepdims=True)
            lifted[which, :, at] = jnp.exp(values - top)
            tops[which : which + 1, at] = top


def last_kernel(nc, nx, place, got, lifted, tops, rows, grads):
    count = got.shape[2]
    pool, dim = grads.shape
    pieces = []
    for i in range(nc * nx):
        c, k = divmod(i, nx)
        at = slice(i * count, (i + 1) * count)
        stats = got[(place[1] + k) % nx * nc + (place[0] + c) % nc]
        weight_s = logit_scale * jnp.exp(tops[0:1, at] - stats[0:1]) / stats[1:2]
        weight_t = logit_scale * jnp.exp(tops[1:2, at] - stats[2:3]) / stats[3:4]
        grad = weight_s * lifted[0, :, at] - weight_t * lifted[1, :, at]
        pieces.append(jnp.concatenate(bf16_parts(grad), axis=0))
    total = jnp.dot(
        jnp.concatenate(pieces, axis=1), rows[:, :dim], preferred_element_type=f32
    )
    grads[...] = total[:pool] + total[pool:]


vmem = pl.BlockSpec(memory_space=pltpu.VMEM)


def first_buffer(queries, teacher, sizes):
    ny, nzl, group, nzh, pool = sizes
    own, dim = queries.shape
    return pl.pallas_call(
        functools.partial(first_kernel, sizes),
        out_shape=jax.ShapeDtypeStruct((nzh * nzl, own, ny * group * pool + dim), bf16),
        in_specs=[pl.BlockSpec(memory_space=pltpu.HBM)] * 2,
        out_specs=vmem,
        scratch_shapes=[
            pltpu.VMEM(queries.shape, bf16),
            pltpu.VMEM(teacher.shape, bf16),
            pltpu.SemaphoreType.DMA((2,)),
        ],
        compiler_params=pltpu.CompilerParams(vmem_limit_bytes=60 * 2**20),
        cost_estimate=pl.CostEstimate(flops=0, bytes_accessed=2**20, transcendentals=0),
    )(queries, teacher)


def place_of():
    return jnp.stack([lax.axis_index("core"), lax.axis_index("x")]).astype(jnp.int32)


def laid_out(got, sizes):
    ny, width, nc, nx, pool, dim = sizes
    count, group = ny * width, nc * nx
    place = place_of()
    lifted = jax.ShapeDtypeStruct((count, group * pool), bf16)
    row = jax.ShapeDtypeStruct((count, dim + nc * pool), bf16)
    mine = jax.ShapeDtypeStruct((count, nc * pool), bf16)
    block = jax.ShapeDtypeStruct((count, dim), bf16)
    stats = jax.ShapeDtypeStruct((width, count), f32)
    return pl.pallas_call(
        functools.partial(layout_kernel, nc, nx),
        out_shape=(block, lifted, lifted, stats, mine) + (row,) * (nx - 1),
        in_specs=[pl.BlockSpec(memory_space=pltpu.SMEM), vmem],
        out_specs=(vmem,) * (4 + nx),
        compiler_params=pltpu.CompilerParams(vmem_limit_bytes=16 * 2**20),
        cost_estimate=pl.CostEstimate(
            flops=30 * 10**9, bytes_accessed=32 * 2**20, transcendentals=0
        ),
    )(place, got)


def local_parts(block, high, low, stats, near, far, ny):
    count, dim = block.shape
    return pl.pallas_call(
        parts_kernel,
        out_shape=jax.ShapeDtypeStruct((ny, count // ny, 2 * dim + count), f32),
        in_specs=[vmem] * 6,
        out_specs=vmem,
        compiler_params=pltpu.CompilerParams(vmem_limit_bytes=16 * 2**20),
        cost_estimate=pl.CostEstimate(
            flops=10 * count * high.shape[1] * dim,
            bytes_accessed=4 * 2**20,
            transcendentals=count * high.shape[1],
        ),
    )(block, high, low, stats, near.reshape(-1, dim), far.reshape(-1, dim))


def simple_call(kernel, out, scalars, arrays, flops=0):
    smem = pl.BlockSpec(memory_space=pltpu.SMEM)
    return pl.pallas_call(
        kernel,
        out_shape=out,
        in_specs=[smem] * len(scalars) + [vmem] * len(arrays),
        out_specs=(vmem,) * len(out) if isinstance(out, tuple) else vmem,
        compiler_params=pltpu.CompilerParams(vmem_limit_bytes=16 * 2**20),
        cost_estimate=pl.CostEstimate(flops=flops, bytes_accessed=2**16, transcendentals=0),
    )(*scalars, *arrays)


def per_device(queries, passages, teacher):
    own, dim = queries.shape
    pool = passages.shape[0]
    ny, nzl, nc, nx, nzh = (lax.axis_size(a) for a in names)
    nz, group = nzh * nzl, nc * nx

    near = [from_next(passages, "x", k) for k in range(1, nx)]

    got = exchange(first_buffer(queries, teacher, (ny, nzl, group, nzh, pool)), z_axes)
    got, *near = lax.optimization_barrier((got, *near))
    width, count = nz * own, ny * nz * own
    got = got.reshape(width, -1)
    tiles = [got[:, i * group * pool : (i + 1) * group * pool] for i in range(ny)]
    sent = jnp.stack([jnp.concatenate([t, got[:, ny * group * pool :]], axis=1) for t in tiles])
    got = exchange(sent, "y")
    *near, _ = lax.optimization_barrier((*near, sent))
    near = jnp.stack([passages, *near])
    far = from_next(near, "core", 1)
    block, high, low, stats, *rows = laid_out(got.reshape(count, -1), (ny, width, nc, nx, pool, dim))
    parts = local_parts(block, high, low, stats, near, far, ny)

    for k in range(2, nx):
        rows[k] = from_next(rows[k], "x", k)

    z_at = lax.axis_index("y") * width + lax.axis_index(z_axes) * own
    extra = 4 // min(own, 4) * count
    sent = simple_call(
        middle_kernel,
        jax.ShapeDtypeStruct((nz, own, 2 * dim + extra), f32),
        [lax.axis_index("y").astype(jnp.int32)[None]],
        [exchange(parts, "y")],
    )
    got = exchange(sent, z_axes)
    rows[0] = jnp.concatenate([block, rows[0]], axis=1)
    *rows, _ = lax.optimization_barrier((*rows, sent))
    rows[1] = from_next(rows[1], "x", 1)

    kept = jnp.stack([r[:, : dim + pool] for r in rows])
    away = jnp.stack([jnp.concatenate([r[:, :dim], r[:, dim + pool :]], axis=1) for r in rows])
    every_row = jnp.concatenate([kept, from_next(away, "core", 1)]).reshape(group * count, dim + pool)

    lifted = jax.ShapeDtypeStruct((2, pool, group * count), f32)
    tops = jax.ShapeDtypeStruct((2, group * count), f32)
    sets = simple_call(own_kernel, (lifted, tops), [], [passages, every_row], flops=2 * pool * group * count * dim)
    got, *sets = lax.optimization_barrier((got, *sets))
    every = simple_call(
        functools.partial(after_kernel, dim), jax.ShapeDtypeStruct((group, 4, count), f32), [], [got]
    )
    got, _ = lax.optimization_barrier((got, every))
    every = exchange(every, ("x", "core"))
    query_grad = simple_call(
        functools.partial(query_kernel, count),
        jax.ShapeDtypeStruct((own, dim), f32),
        [z_at.astype(jnp.int32)[None]],
        [got],
    )

    passage_grad = simple_call(
        functools.partial(last_kernel, nc, nx),
        jax.ShapeDtypeStruct((pool, dim), f32),
        [place_of()],
        [every, *sets, every_row],
    )
    return query_grad, passage_grad


def solution(mesh):
    shape = sizes if mesh.devices.size == 512 else (2,) * 5
    fine = Mesh(mesh.devices.reshape(shape), names)
    placed = P(names, None)
    return jax.shard_map(
        per_device,
        mesh=fine,
        in_specs=(placed, placed, placed),
        out_specs=(placed, placed),
        check_vma=False,
    )
```
